256 devices in a mesh: dp: 32 (over x_lo, z, core), mp: 8 (over y, x_hi).
Axes of the slice: x: 4 (x_hi: 2, x_lo: 2; x = x_hi * 2 + x_lo), y: 4, z: 8, core: 2. Of those that a mesh axis runs over, the one named last changes fastest.
Arguments:
- video_feats: bfloat16 [8192, 3200], P('dp'), may hold values from -18 to 18
- text_feats: bfloat16 [8192, 512], P('dp'), may hold values from -11 to 11
- weight_in: bfloat16 [3200, 6400], P(None, 'mp'), may hold values from -0.109375 to 0.109375
- weight_out: bfloat16 [6400, 512], P('mp'), may hold values from -0.07625 to 0.07625
- logit_scale: float32 [1], replicated, may hold values from 20 to 50
Outputs:
- loss: float32 [1], replicated
- grad_in: float32 [3200, 6400], P('dp', 'mp')
- grad_out: float32 [6400, 512], P('mp', 'dp')
The draws below stay inside these ranges and needn't reach their ends.
All inputs are finite; a program needn't handle non-finite values.
Results may differ from the reference program's by a relative error of at most 0.015.
Values may be sent and summed in bfloat16 or wider, within the bound.
No kernel may reach another device: no remote copies, remote signals or barrier semaphores. Data moves between devices by JAX's collectives and lax.ppermute only.
A program may use at most 128 MiB of HBM per device.

```python
import math
import jax
import jax.numpy as jnp
from jax import lax

D_IN = 3200
HID = 6400
EMB = 512
TOK_DEV = 256
TOKENS = 8192


def shared_direction(key):
    return jnp.clip(jax.random.normal(key, (EMB,), jnp.float32), -6.0, 6.0)


def draw_video_feats(key, part):
    key = jax.random.fold_in(key, 11)
    position = jnp.arange(TOKENS).astype(jnp.float32) / (TOKENS - 1)
    noise = jnp.clip(jax.random.normal(key, (TOKENS, D_IN), jnp.float32), -6.0, 6.0)
    row_scale = 0.3 * jnp.power(10.0, position)
    return (noise * row_scale[:, None]).astype(jnp.bfloat16)


def draw_text_feats(key, part):
    direction = shared_direction(key)
    key = jax.random.fold_in(key, 12)
    index = jnp.arange(TOKENS)
    shard_frac = (index // TOK_DEV).astype(jnp.float32) / max(TOKENS // TOK_DEV - 1, 1)
    inner_frac = (index % TOK_DEV).astype(jnp.float32) / (TOK_DEV - 1)
    mixing = 0.5 * shard_frac + 0.5 * inner_frac
    noise = jnp.clip(jax.random.normal(key, (TOKENS, EMB), jnp.float32), -6.0, 6.0)
    along = 0.25 + 0.5 * mixing
    rest = jnp.sqrt(1.0 - along * along)
    return (along[:, None] * direction[None, :] + rest[:, None] * noise).astype(jnp.bfloat16)


def draw_weight_out(key, part):
    direction = shared_direction(key)
    key = jax.random.fold_in(key, 13)
    noise = jnp.clip(jax.random.normal(key, (HID, EMB), jnp.float32), -6.0, 6.0)
    return (noise / jnp.sqrt(float(HID)) + 1.3 / HID * direction[None, :]).astype(jnp.bfloat16)


def level_of(own_key, shape, cuts, least, largest):
    loudness, own = 1.0, jax.random.fold_in(own_key, 6)
    for dim, blocks in cuts:
        draws = jnp.exp(jax.random.uniform(jax.random.fold_in(own, dim), (blocks,), jnp.float32, least / len(cuts), largest / len(cuts)))
        loudness = loudness * jnp.repeat(draws, shape[dim] // blocks).reshape([-1 if axis == dim else 1 for axis in range(len(shape))])
    return loudness


def centred(own_key, dims, width, bound, cuts=(), kind=jnp.bfloat16):
    values = width * jax.random.normal(own_key, dims, jnp.float32)
    if cuts:
        values = values * level_of(own_key, dims, cuts, -0.22, 0.18)
    return jnp.clip(values, -bound, bound).astype(kind)


def setup_inputs(seed: int = 0) -> dict:
    streams_of = jax.random.split(jax.random.key(seed), 6)
    video_feats = draw_video_feats(jax.random.fold_in(streams_of[5], 71), 0)
    text_feats = draw_text_feats(jax.random.fold_in(streams_of[5], 71), 0)
    weight_in = centred(streams_of[2], (D_IN, HID), D_IN ** -0.5, 0.109375, ((1, 8),))
    weight_out = draw_weight_out(jax.random.fold_in(streams_of[5], 71), 0)
    logit_scale = jnp.clip(jnp.exp(jax.random.uniform(streams_of[4], (1,), jnp.float32, math.log(20.0), math.log(50.0))), 20.0, 50.0)
    return {"video_feats": video_feats, "text_feats": text_feats, "weight_in": weight_in, "weight_out": weight_out, "logit_scale": logit_scale}


EPS = 1e-06
GELU_C = 0.7978845608
GELU_K = 0.044715

def gelu_parts(values):
    inner = GELU_C * (values + GELU_K * values * values * values)
    tanh_val = jnp.tanh(inner)
    gelu_val = 0.5 * values * (1.0 + tanh_val)
    gelu_der = 0.5 * (1.0 + tanh_val) + 0.5 * values * (1.0 - tanh_val * tanh_val) * GELU_C * (1.0 + 3.0 * GELU_K * values * values)
    return (gelu_val, gelu_der)

def reference(video_feats, text_feats, weight_in, weight_out, logit_scale):
    batch_total = video_feats.shape[0]
    preact = jnp.dot(video_feats, weight_in, preferred_element_type=jnp.float32)
    gelu_val, gelu_der = gelu_parts(preact)
    hidden = gelu_val.astype(jnp.bfloat16)
    projected = jnp.dot(hidden, weight_out, preferred_element_type=jnp.float32)
    inv_norm = lax.rsqrt(lax.optimization_barrier(jnp.sum(projected * projected, axis=-1, keepdims=True)) + EPS)
    unit_emb = projected * inv_norm
    video_emb = unit_emb.astype(jnp.bfloat16)
    text_float = text_feats.astype(jnp.float32)
    text_emb = (text_float * lax.rsqrt(lax.optimization_barrier(jnp.sum(text_float * text_float, axis=-1, keepdims=True)) + EPS)).astype(jnp.bfloat16)
    scale_val = logit_scale[0]
    block_count = batch_total // TOK_DEV
    video_blocks = video_emb.reshape(block_count, TOK_DEV, EMB)

    def sums_step(col_acc, block):
        expo = jnp.exp(scale_val * jnp.dot(block, text_emb.T, preferred_element_type=jnp.float32))
        return (col_acc + lax.optimization_barrier(jnp.sum(expo, axis=0)), lax.optimization_barrier(jnp.sum(expo, axis=1)))
    col_sum, row_blocks = lax.scan(sums_step, jnp.zeros((batch_total,), jnp.float32), video_blocks)
    row_sum = row_blocks.reshape(batch_total)
    positive = scale_val * lax.optimization_barrier(jnp.sum(video_emb.astype(jnp.float32) * text_emb.astype(jnp.float32), axis=-1))
    loss = (jnp.sum(jnp.log(row_sum)) + jnp.sum(jnp.log(col_sum)) - 2.0 * jnp.sum(positive)) / (2.0 * batch_total)

    def grad_block(pieces):
        block, row_piece = pieces
        expo = jnp.exp(scale_val * jnp.dot(block, text_emb.T, preferred_element_type=jnp.float32))
        pair_weight = (expo / row_piece[:, None] + expo / col_sum[None, :]).astype(jnp.bfloat16)
        return jnp.dot(pair_weight, text_emb, preferred_element_type=jnp.float32)
    weighted = lax.map(grad_block, (video_blocks, row_blocks)).reshape(batch_total, EMB)
    grad_emb = 0.5 * scale_val * weighted - scale_val * text_emb.astype(jnp.float32)
    grad_proj = (inv_norm * (grad_emb - unit_emb * lax.optimization_barrier(jnp.sum(unit_emb * grad_emb, axis=-1, keepdims=True)))).astype(jnp.bfloat16)
    grad_out = jnp.dot(hidden.T, grad_proj, preferred_element_type=jnp.float32)
    grad_hidden = jnp.dot(grad_proj, weight_out.T, preferred_element_type=jnp.float32)
    grad_pre = (grad_hidden * gelu_der).astype(jnp.bfloat16)
    grad_in = jnp.dot(video_feats.T, grad_pre, preferred_element_type=jnp.float32)
    return (loss.reshape(1), grad_in, grad_out)
```

```python
import jax
import jax.numpy as jnp
from jax import lax
from jax.sharding import Mesh, PartitionSpec as P

EPS = 1e-06
GELU_C = 0.7978845608
GELU_K = 0.044715
MP = ("y", "x_hi")
DP = ("x_lo", "z", "core")
PLANE = ("core", "x_lo", "y", "x_hi")
BF = jnp.bfloat16
F32 = jnp.float32


def gelu_val(values, tanh_val):
    return 0.5 * values * (1.0 + tanh_val)


def gelu_der(values, tanh_val):
    return 0.5 * (1.0 + tanh_val) + 0.5 * values * (1.0 - tanh_val * tanh_val) * GELU_C * (
        1.0 + 3.0 * GELU_K * values * values
    )


def gelu_tanh(values):
    return jnp.tanh(GELU_C * (values + GELU_K * values * values * values))


def swap(value, axis):
    return lax.ppermute(value, axis, [(0, 1), (1, 0)])


def ordered(own, other, index):
    return jnp.where(index == 0, jnp.stack([own, other]), jnp.stack([other, own]))


def exchange(value, axis):
    return lax.all_to_all(value, axis, 0, 0)


def spread(value, axis):
    count = lax.axis_size(axis)
    return exchange(jnp.broadcast_to(value[None], (count,) + value.shape), axis)


def split3(value):
    first = value.astype(BF).astype(F32)
    second = (value - first).astype(BF).astype(F32)
    third = value - first - second
    return first, second, third


def on_device(video_feats, text_feats, weight_in, weight_out, logit_scale):
    rows = video_feats.shape[0]
    d_in = video_feats.shape[1]
    hid = weight_in.shape[1]
    emb = text_feats.shape[1]
    mp_count = lax.axis_size(MP)
    z_count = lax.axis_size("z")
    own_rows = rows // mp_count
    mp_index = lax.axis_index(MP)
    x_index = lax.axis_index("x_lo")
    c_index = lax.axis_index("core")
    batch_total = rows * lax.axis_size(DP)
    scale_val = logit_scale[0]

    text_float = text_feats.astype(F32)
    text_emb = (
        text_float * lax.rsqrt(jnp.sum(text_float * text_float, axis=-1, keepdims=True) + EPS)
    ).astype(BF)
    pair = ordered(text_emb, swap(text_emb, "x_lo"), x_index)
    text_cols = ordered(pair, swap(pair, "core"), c_index).reshape(4 * rows, emb)

    in_rows = d_in // lax.axis_size(DP)
    feats_t = video_feats.T.reshape(2, z_count, 2, in_rows, rows).transpose(2, 0, 1, 3, 4)
    keep = lax.dynamic_index_in_dim(feats_t, c_index, 0, False)
    give = lax.dynamic_index_in_dim(feats_t, 1 - c_index, 0, False)
    feats_c = ordered(keep, swap(give, "core"), c_index)
    keep = lax.dynamic_index_in_dim(feats_c, x_index, 1, False)
    give = lax.dynamic_index_in_dim(feats_c, 1 - x_index, 1, False)
    feats_q = ordered(keep, swap(give, "x_lo"), x_index)

    preact = jnp.dot(video_feats, weight_in, preferred_element_type=F32)
    hidden = gelu_val(preact, gelu_tanh(preact)).astype(BF)
    partial_value = jnp.dot(hidden, weight_out, preferred_element_type=F32).astype(BF)
    pre_bf = preact.astype(BF)
    pre_pair = ordered(pre_bf, swap(pre_bf, "x_lo"), x_index)
    pre_all = ordered(pre_pair, swap(pre_pair, "core"), c_index).reshape(4 * rows, hid)

    got = exchange(partial_value.reshape(mp_count, own_rows, emb), MP)
    projected = jnp.sum(got.astype(F32), axis=0)
    inv_norm = lax.rsqrt(jnp.sum(projected * projected, axis=-1, keepdims=True) + EPS)
    unit_emb = projected * inv_norm
    video_emb = unit_emb.astype(BF)
    video_rows = spread(video_emb, "z").reshape(z_count * own_rows, emb)

    logits = scale_val * lax.dot_general(
        video_rows, text_cols, (((1,), (1,)), ((), ())), preferred_element_type=F32
    )
    expo = jnp.exp(logits)
    row_part = jnp.sum(expo, axis=1)
    col_part = jnp.sum(expo, axis=0)
    col_sum = jnp.sum(spread(col_part.reshape(-1, 128), PLANE), axis=0).reshape(-1)
    first = jnp.dot(expo.astype(BF), text_cols, preferred_element_type=F32)
    second = jnp.dot(
        (expo / col_sum[None, :]).astype(BF), text_cols, preferred_element_type=F32
    )
    row_hi = row_part.astype(BF).astype(F32)
    row_lo = row_part - row_hi
    lane = lax.broadcasted_iota(jnp.int32, (1, 128), 1)
    row_lanes = jnp.where(lane < 64, row_hi[:, None], row_lo[:, None])
    packed = jnp.concatenate([first, second, row_lanes], axis=1).astype(BF)
    back = exchange(packed.reshape(z_count, own_rows, 2 * emb + 128), "z")
    back = jnp.sum(back.astype(F32), axis=0)
    row_sum = back[:, 2 * emb : 2 * emb + 1] + back[:, 2 * emb + 64 : 2 * emb + 65]
    weighted = back[:, :emb] / row_sum + back[:, emb : 2 * emb]

    text_own = lax.dynamic_slice_in_dim(text_emb, mp_index * own_rows, own_rows, 0).astype(F32)
    positive = scale_val * jnp.sum(video_emb.astype(F32) * text_own, axis=-1)
    loss_piece = (
        jnp.sum(jnp.log(row_sum))
        - 2.0 * jnp.sum(positive)
        + jnp.sum(jnp.log(col_sum)) / lax.axis_size(PLANE)
    )

    grad_emb = 0.5 * scale_val * weighted - scale_val * text_own
    grad_proj = inv_norm * (
        grad_emb - unit_emb * jnp.sum(unit_emb * grad_emb, axis=-1, keepdims=True)
    )
    a, b, c = split3(loss_piece)
    lane = lax.broadcasted_iota(jnp.int32, (1, emb), 1)
    loss_row = jnp.where(lane == 0, a, jnp.where(lane == 1, b, jnp.where(lane == 2, c, 0.0)))
    sent = jnp.concatenate([grad_proj, loss_row], axis=0).astype(BF)
    grads = spread(sent, PLANE)
    loss_piece = jnp.sum(grads[:, own_rows, :].astype(F32))
    gproj = grads[:, :own_rows, :].reshape(4 * rows, emb)

    pre_f = pre_all.astype(F32)
    tanh_all = gelu_tanh(pre_f)
    hidden_all = gelu_val(pre_f, tanh_all).astype(BF)
    grad_hidden = lax.dot_general(
        gproj, weight_out, (((1,), (1,)), ((), ())), preferred_element_type=F32
    )
    grad_pre = (grad_hidden * gelu_der(pre_f, tanh_all)).astype(BF)
    out_term = lax.dot_general(gproj, hidden_all, (((0,), (0,)), ((), ())), preferred_element_type=F32)
    out_cols = emb // lax.axis_size(DP)
    out_term = out_term.reshape(2, z_count, 2, out_cols, hid)
    out_term = lax.dynamic_index_in_dim(out_term, x_index, 0, False)
    out_term = lax.dynamic_index_in_dim(out_term, c_index, 1, False)
    grad_pre4 = grad_pre.reshape(2, 2, rows, hid)
    in_term = 0.0
    for core in range(2):
        for x in range(2):
            in_term = in_term + jnp.dot(
                feats_q[x, core].reshape(z_count * in_rows, rows),
                grad_pre4[core, x],
                preferred_element_type=F32,
            )
    a, b, c = split3(loss_piece)
    lane = lax.broadcasted_iota(jnp.int32, (1, 1, hid), 2)
    loss_row = jnp.where(lane == 0, a, jnp.where(lane == 1, b, jnp.where(lane == 2, c, 0.0)))
    loss_row = jnp.broadcast_to(loss_row, (z_count, 1, hid))
    packed = jnp.concatenate(
        [out_term.astype(BF), in_term.reshape(z_count, in_rows, hid).astype(BF), loss_row.astype(BF)],
        axis=1,
    )
    final = jnp.sum(exchange(packed, "z").astype(F32), axis=0)
    grad_out = final[:out_cols].T
    grad_in = final[out_cols : out_cols + in_rows]
    loss = jnp.sum(final[out_cols + in_rows, :3]) / (2.0 * batch_total)
    return (loss.reshape(1), grad_in, grad_out)


def solution(mesh):
    fine = Mesh(mesh.devices.reshape(2, -1, 2, mesh.devices.shape[1] // 2, 2), DP + MP)
    in_specs = (P(DP, None), P(DP, None), P(None, MP), P(MP, None), P())
    out_specs = (P(), P(DP, MP), P(MP, DP))
    return jax.shard_map(
        on_device, mesh=fine, in_specs=in_specs, out_specs=out_specs, check_vma=False
    )
```

```python
import functools

import jax
import jax.numpy as jnp
from jax import lax
from jax.experimental import pallas as pl
from jax.experimental.pallas import tpu as pltpu
from jax.sharding import Mesh, PartitionSpec as P

EPS = 1e-06
GELU_C = 0.7978845608
GELU_K = 0.044715
MP = ("y", "x_hi")
DP = ("x_lo", "z", "core")
PLANE = ("core", "x_lo", "y", "x_hi")
BF = jnp.bfloat16
F32 = jnp.float32
LANES = 128
OUT_COLS = 16
MIB = 1 << 20
NT = (((1,), (1,)), ((), ()))


def gelu_val(values, tanh_val):
    return 0.5 * values * (1.0 + tanh_val)


def gelu_der(values, tanh_val):
    return 0.5 * (1.0 + tanh_val) + 0.5 * values * (1.0 - tanh_val * tanh_val) * GELU_C * (
        1.0 + 3.0 * GELU_K * values * values
    )


def gelu_tanh(values):
    return jnp.tanh(GELU_C * (values + GELU_K * values * values * values))


def swap(value, axis):
    return lax.ppermute(value, axis, [(0, 1), (1, 0)])


def exchange(value, axis):
    return lax.all_to_all(value, axis, 0, 0)


def split3(value):
    first = value.astype(BF).astype(F32)
    second = (value - first).astype(BF).astype(F32)
    return first, second, value - first - second


def call(kernel, outs, vmem, cost, *args, scalars=0, scratch=()):
    specs = [pl.BlockSpec(memory_space=pltpu.SMEM)] * scalars
    specs += [pl.BlockSpec(memory_space=pltpu.VMEM)] * (len(args) - scalars)
    moved = sum(a.size * a.dtype.itemsize for a in args)
    return pl.pallas_call(
        kernel,
        out_shape=[jax.ShapeDtypeStruct(s, d) for s, d in outs],
        in_specs=specs,
        out_specs=[pl.BlockSpec(memory_space=pltpu.VMEM)] * len(outs),
        scratch_shapes=list(scratch),
        compiler_params=pltpu.CompilerParams(vmem_limit_bytes=vmem * MIB),
        cost_estimate=pl.CostEstimate(flops=cost, bytes_accessed=moved, transcendentals=0),
    )(*args)


def text_kernel(text_ref, out_ref):
    text = text_ref[...].astype(F32)
    out_ref[...] = (text * lax.rsqrt(jnp.sum(text * text, axis=-1, keepdims=True) + EPS)).astype(BF)


def feats_kernel(where_ref, feats_ref, out_ref):
    x_index, c_index = where_ref[0], where_ref[1]
    width = feats_ref.shape[1]
    z_count = out_ref.shape[3] // LANES
    chunk = width // (4 * z_count)
    source = lax.broadcasted_iota(jnp.int32, (2 * LANES, LANES), 0)
    target = lax.broadcasted_iota(jnp.int32, (2 * LANES, LANES), 1)
    inside = (target >= OUT_COLS) & (target < OUT_COLS + chunk)
    for x in range(2):
        for c in range(2):
            for z in range(z_count):
                begin = (x * 2 * z_count + z * 2 + c) * chunk
                window = min(begin // LANES * LANES, width - 2 * LANES)
                shift = begin - window - OUT_COLS
                move = jnp.where(inside & (source == target + shift), 1.0, 0.0).astype(BF)
                piece = jnp.dot(
                    feats_ref[:, window : window + 2 * LANES], move, preferred_element_type=F32
                )
                out_ref[x ^ x_index, c ^ c_index, :, z * LANES : (z + 1) * LANES] = piece.astype(BF)


def unit_kernel(got_ref, unit_ref, inv_ref, spread_ref):
    projected = jnp.sum(got_ref[...].astype(F32), axis=0)
    inv_norm = lax.rsqrt(jnp.sum(projected * projected, axis=-1, keepdims=True) + EPS)
    unit = projected * inv_norm
    unit_ref[...] = unit
    inv_ref[...] = jnp.broadcast_to(inv_norm, inv_ref.shape)
    spread_ref[...] = jnp.broadcast_to(unit.astype(BF)[None], spread_ref.shape)


def logits_kernel(where_ref, scale_ref, video_ref, *refs):
    text_refs, (expo_ref, first_ref, lanes_ref, spread_ref, col_ref) = refs[:4], refs[4:]
    x_index, c_index = where_ref[0], where_ref[1]
    scale_val = scale_ref[0]
    z_count, own_rows, emb = video_ref.shape
    video = video_ref[...].reshape(z_count * own_rows, emb)
    first = jnp.zeros((z_count * own_rows, emb), F32)
    row_part = jnp.zeros((z_count * own_rows, 1), F32)
    for block in range(4):
        rx, rc = block // 2, block % 2
        text = text_refs[block][...]
        expo = jnp.exp(scale_val * lax.dot_general(video, text, NT, preferred_element_type=F32))
        expo_ref[block] = expo
        row_part += jnp.sum(expo, axis=1, keepdims=True)
        col_part = jnp.sum(expo, axis=0, keepdims=True)
        place = ((rc ^ c_index) * 2 + (rx ^ x_index)) * 2
        for half in range(2):
            col_ref[pl.ds(place + half, 1), :] = col_part[:, half * LANES : (half + 1) * LANES]
        first += jnp.dot(expo.astype(BF), text, preferred_element_type=F32)
    first_ref[...] = first.astype(BF).reshape(first_ref.shape)
    row_hi = row_part.astype(BF).astype(F32)
    lane = lax.broadcasted_iota(jnp.int32, (z_count * own_rows, LANES), 1)
    both = jnp.where(lane < LANES // 2, row_hi, row_part - row_hi)
    lanes_ref[...] = both.astype(BF).reshape(lanes_ref.shape)
    spread_ref[...] = jnp.broadcast_to(col_ref[...][None], spread_ref.shape)


def weights_kernel(where_ref, got_ref, expo_ref, first_ref, lanes_ref, *refs):
    text_refs, (packed_ref, log_ref, inv_ref) = refs[:4], refs[4:]
    x_index, c_index = where_ref[0], where_ref[1]
    z_count, own_rows, emb = first_ref.shape
    col_sum = jnp.sum(got_ref[...], axis=0)
    log_ref[...] = jnp.log(col_sum)
    inv_ref[...] = 1.0 / col_sum
    second = jnp.zeros((z_count * own_rows, emb), F32)
    for block in range(4):
        rx, rc = block // 2, block % 2
        place = ((rc ^ c_index) * 2 + (rx ^ x_index)) * 2
        for half in range(2):
            lanes = slice(half * LANES, (half + 1) * LANES)
            weight = expo_ref[block, :, lanes] * inv_ref[pl.ds(place + half, 1), :]
            second += jnp.dot(
                weight.astype(BF), text_refs[block][lanes, :], preferred_element_type=F32
            )
    packed_ref[:, :, :emb] = first_ref[...]
    packed_ref[:, :, emb : 2 * emb] = second.astype(BF).reshape(first_ref.shape)
    packed_ref[:, :, 2 * emb :] = lanes_ref[...]


def proj_kernel(where_ref, scale_ref, back_ref, unit_ref, inv_ref, text_ref, log_ref, out_ref):
    scale_val = scale_ref[0]
    own_rows, emb = unit_ref.shape
    back = jnp.sum(back_ref[...].astype(F32), axis=0)
    half = 2 * emb + LANES // 2
    row_sum = back[:, 2 * emb : 2 * emb + 1] + back[:, half : half + 1]
    weighted = back[:, :emb] / row_sum + back[:, emb : 2 * emb]
    text = text_ref[where_ref[2]].astype(F32)
    unit = unit_ref[...]
    positive = scale_val * jnp.sum(unit.astype(BF).astype(F32) * text, axis=-1, keepdims=True)
    rows_piece = jnp.sum(jnp.log(row_sum) - 2.0 * positive, axis=0, keepdims=True)
    cols_piece = jnp.sum(jnp.sum(log_ref[...], axis=0, keepdims=True), axis=1, keepdims=True)
    a, b, c = split3(rows_piece + cols_piece / out_ref.shape[0])
    grad_emb = 0.5 * scale_val * weighted - scale_val * text
    grad_proj = inv_ref[:, :1] * (
        grad_emb - unit * jnp.sum(unit * grad_emb, axis=-1, keepdims=True)
    )
    lane = lax.broadcasted_iota(jnp.int32, (own_rows, LANES), 1)
    row = lax.broadcasted_iota(jnp.int32, (own_rows, LANES), 0)
    loss = jnp.where(lane == 0, a, jnp.where(lane == 1, b, jnp.where(lane == 2, c, 0.0)))
    loss = jnp.where(row == 0, loss, 0.0)
    sent = jnp.concatenate([grad_proj, loss], axis=1).astype(BF)
    out_ref[...] = jnp.broadcast_to(sent[None], out_ref.shape)


def gelu_kernel(*refs):
    pre_refs, (hidden_ref, der_ref) = refs[:4], refs[4:]
    for block in range(4):
        pre = pre_refs[block][...].astype(F32)
        tanh_val = gelu_tanh(pre)
        hidden_ref[block] = gelu_val(pre, tanh_val).astype(BF)
        der_ref[block] = gelu_der(pre, tanh_val).astype(BF)


def grads_kernel(where_ref, grads_ref, hidden_ref, der_ref, weight_ref, *refs):
    feats_refs, (out_ref,) = refs[:4], refs[4:]
    x_index, c_index = where_ref[0], where_ref[1]
    _, mp_count, own_rows, wide = grads_ref.shape
    emb = wide - LANES
    hid = weight_ref.shape[0]
    z_count = out_ref.shape[0]
    rows = mp_count * own_rows
    source = lax.broadcasted_iota(jnp.int32, (emb, LANES), 0)
    target = lax.broadcasted_iota(jnp.int32, (emb, LANES), 1)
    column = x_index * (emb // 2) + (target // OUT_COLS) * (2 * OUT_COLS) + c_index * OUT_COLS
    pick = jnp.where(source == column + target % OUT_COLS, 1.0, 0.0).astype(BF)
    grads, picked = [], []
    for block in range(4):
        rx, rc = block // 2, block % 2
        part = grads_ref[(rc ^ c_index) * 2 + (rx ^ x_index), :, :, :emb].reshape(rows, emb)
        grads.append(part)
        picked.append(jnp.dot(part, pick, preferred_element_type=F32).astype(BF))
    loss = jnp.sum(grads_ref[:, :, 0, emb:].astype(F32).reshape(4 * mp_count, LANES), axis=0, keepdims=True)
    loss = jnp.sum(loss, axis=1, keepdims=True)
    parts = 2
    step = hid // parts
    lane = lax.broadcasted_iota(jnp.int32, (step, LANES), 1)
    row = lax.broadcasted_iota(jnp.int32, (step, LANES), 0)
    a, b, c = split3(loss)
    extra = jnp.where(row == 0, a, jnp.where(row == 1, b, jnp.where(row == 2, c, 0.0)))
    extra = jnp.where(lane == LANES - 1, extra, 0.0)
    for part in range(parts):
        span = slice(part * step, (part + 1) * step)
        total = jnp.zeros((step, z_count * LANES), F32)
        outer = jnp.zeros((step, LANES), F32)
        for block in range(4):
            grad_hidden = lax.dot_general(
                weight_ref[span, :], grads[block], NT, preferred_element_type=F32
            )
            grad_pre = (grad_hidden * der_ref[block, span, :].astype(F32)).astype(BF)
            total += jnp.dot(grad_pre, feats_refs[block][...], preferred_element_type=F32)
            outer += jnp.dot(hidden_ref[block, span, :], picked[block], preferred_element_type=F32)
        for z in range(z_count):
            moved = outer if z == 0 else pltpu.roll(outer, LANES - z * OUT_COLS, 1)
            value = jnp.where(lane < OUT_COLS, moved, total[:, z * LANES : (z + 1) * LANES])
            if part == 0:
                value = jnp.where(lane == LANES - 1, extra, value)
            out_ref[z, span, :] = value.astype(BF)


def final_kernel(got_ref, in_ref, out_ref, loss_ref, *, batch_total):
    total = jnp.sum(got_ref[...].astype(F32), axis=0)
    turned = total.T
    in_rows = in_ref.shape[0]
    out_ref[...] = turned[:OUT_COLS]
    in_ref[...] = turned[OUT_COLS : OUT_COLS + in_rows]
    loss = jnp.sum(total[:3, LANES - 1 :], axis=0, keepdims=True) / (2.0 * batch_total)
    loss_ref[...] = loss


def on_device(video_feats, text_feats, weight_in, weight_out, logit_scale):
    rows, d_in = video_feats.shape
    hid, emb = weight_out.shape
    mp_count = lax.axis_size(MP)
    z_count = lax.axis_size("z")
    plane = lax.axis_size(PLANE)
    own_rows = rows // mp_count
    batch_total = rows * lax.axis_size(DP)
    where = jnp.stack([lax.axis_index("x_lo"), lax.axis_index("core"), lax.axis_index(MP)])
    where = where.astype(jnp.int32)

    pre_t = lax.dot_general(weight_in, video_feats, (((0,), (1,)), ((), ())), preferred_element_type=F32)
    hidden_t = gelu_val(pre_t, gelu_tanh(pre_t)).astype(BF)
    partial_value = lax.dot_general(
        hidden_t, weight_out, (((0,), (0,)), ((), ())), preferred_element_type=F32
    ).astype(BF)
    got = exchange(partial_value.reshape(mp_count, own_rows, emb), MP)

    (text_emb,) = call(text_kernel, [((rows, emb), BF)], 8, 10**6, text_feats)
    text_x = swap(text_emb, "x_lo")
    text = (text_emb, swap(text_emb, "core"), text_x, swap(text_x, "core"))

    (feats,) = call(
        feats_kernel, [((2, 2, rows, z_count * LANES), BF)], 16, 10**9, where, video_feats, scalars=1
    )
    feats_x = swap(feats[1], "x_lo")
    feats_q = (feats[0, 0], swap(feats[0, 1], "core"), feats_x[0], swap(feats_x[1], "core"))

    pre_bf = pre_t.astype(BF)
    pre_x = swap(pre_bf, "x_lo")
    pre = (pre_bf, swap(pre_bf, "core"), pre_x, swap(pre_x, "core"))

    unit, inv_norm, video = call(
        unit_kernel,
        [((own_rows, emb), F32), ((own_rows, LANES), F32), ((z_count, own_rows, emb), BF)],
        8, 10**6, got,
    )
    video_rows = exchange(video, "z")
    expo, first, lanes, cols = call(
        logits_kernel,
        [
            ((4, rows, rows), F32),
            ((z_count, own_rows, emb), BF),
            ((z_count, own_rows, LANES), BF),
            ((plane, 8, LANES), F32),
        ],
        16, 10**9, where, logit_scale, video_rows, *text, scalars=2,
        scratch=[pltpu.VMEM((8, LANES), F32)],
    )
    cols = exchange(cols, PLANE)
    packed, logs = call(
        weights_kernel,
        [((z_count, own_rows, 2 * emb + LANES), BF), ((8, LANES), F32)],
        16, 10**9, where, cols, expo, first, lanes, *text, scalars=1,
        scratch=[pltpu.VMEM((8, LANES), F32)],
    )
    back = exchange(packed, "z")
    (sent,) = call(
        proj_kernel, [((plane, own_rows, emb + LANES), BF)], 8, 10**6,
        where, logit_scale, back, unit, inv_norm, text_emb.reshape(mp_count, own_rows, emb), logs,
        scalars=2,
    )
    grads = exchange(sent, PLANE)
    hidden_all, der_all = call(
        gelu_kernel, [((4, hid, rows), BF), ((4, hid, rows), BF)], 24, 3 * 10**9, *pre
    )
    (packed,) = call(
        grads_kernel, [((z_count, hid, LANES), BF)], 40, 6 * 10**9,
        where, grads.reshape(4, mp_count, own_rows, emb + LANES), hidden_all, der_all, weight_out,
        *feats_q, scalars=1,
    )
    final = exchange(packed, "z")
    in_rows = d_in // lax.axis_size(DP)
    grad_in, grad_out, loss = call(
        functools.partial(final_kernel, batch_total=batch_total),
        [((in_rows, hid), F32), ((OUT_COLS, hid), F32), ((1, 1), F32)],
        16, 10**7, final,
    )
    return (loss.reshape(1), grad_in, grad_out.T)


def solution(mesh):
    fine = Mesh(mesh.devices.reshape(2, -1, 2, mesh.devices.shape[1] // 2, 2), DP + MP)
    in_specs = (P(DP, None), P(DP, None), P(None, MP), P(MP, None), P())
    out_specs = (P(), P(DP, MP), P(MP, DP))
    return jax.shard_map(
        on_device, mesh=fine, in_specs=in_specs, out_specs=out_specs, check_vma=False
    )
```

```python
import functools

import jax
import jax.numpy as jnp
from jax import lax
from jax.experimental import pallas as pl
from jax.experimental.pallas import tpu as pltpu
from jax.sharding import Mesh, PartitionSpec as P

EPS = 1e-06
GELU_C = 0.7978845608
GELU_K = 0.044715
MP = ("y", "x_hi")
DP = ("x_lo", "zh", "zl", "core")
CUBE = ("x_lo", "zl", "core")
COLS = ("zh", "y", "x_hi")
SPREAD = ("x_lo", "zl", "y", "x_hi")
BF = jnp.bfloat16
F32 = jnp.float32
LANES = 128
OUT_COLS = 16
MIB = 1 << 20
LIM = (60, 60, 8, 60, 60, 60, 60, 60, 16)
NT = (((1,), (1,)), ((), ()))


def gelu_val(values, tanh_val):
    return 0.5 * values * (1.0 + tanh_val)


def gelu_der(values, tanh_val):
    return 0.5 * (1.0 + tanh_val) + 0.5 * values * (1.0 - tanh_val * tanh_val) * GELU_C * (
        1.0 + 3.0 * GELU_K * values * values
    )


def gelu_tanh(values):
    return jnp.tanh(GELU_C * (values + GELU_K * values * values * values))


def swap(value, axis):
    return lax.ppermute(value, axis, [(0, 1), (1, 0)])


def exchange(value, axis):
    return lax.all_to_all(value, axis, 0, 0)


def split3(value):
    first = value.astype(BF).astype(F32)
    second = (value - first).astype(BF).astype(F32)
    return first, second, value - first - second


def call(kernel, outs, vmem, *args, scalars=0, scratch=(), after=(), raw=False):
    held = [] if raw else list(args[scalars:])
    total = len(args) + len(after)

    def body(*refs):
        outputs = refs[total : total + len(outs)]
        rest = refs[total + len(outs) :]
        if raw:
            kernel(*refs[: len(args)], *outputs, *rest)
            return
        places, sems, rest = rest[: len(held)], rest[len(held)], rest[len(held) + 1 :]
        copies = [
            pltpu.make_async_copy(refs[scalars + i], places[i], sems.at[i])
            for i in range(len(held))
        ]
        for copy in copies:
            copy.start()
        for copy in copies:
            copy.wait()
        kernel(*refs[:scalars], *places, *outputs, *rest)

    places = [pltpu.VMEM(a.shape, a.dtype) for a in held]
    if held:
        places.append(pltpu.SemaphoreType.DMA((len(held),)))
    anywhere = pl.BlockSpec(memory_space=pl.ANY)
    return pl.pallas_call(
        body,
        grid=(1,),
        out_shape=[jax.ShapeDtypeStruct(s, d) for s, d in outs],
        in_specs=[pl.BlockSpec(memory_space=pltpu.SMEM)] * scalars + [anywhere] * (total - scalars),
        out_specs=[whole(s) for s, _ in outs],
        scratch_shapes=[*places, *scratch],
        compiler_params=pltpu.CompilerParams(vmem_limit_bytes=vmem * MIB),
        cost_estimate=pl.CostEstimate(flops=1024, bytes_accessed=1024, transcendentals=0),
    )(*args, *after)


def whole(shape):
    return pl.BlockSpec(shape, lambda i: (0,) * len(shape), pipeline_mode=pl.Buffered(1))


def gate(after, *arrays):
    anywhere = pl.BlockSpec(memory_space=pl.ANY)
    return pl.pallas_call(
        lambda *refs: None,
        out_shape=[jax.ShapeDtypeStruct(a.shape, a.dtype) for a in arrays],
        in_specs=[anywhere] * (len(arrays) + 1),
        out_specs=[anywhere] * len(arrays),
        input_output_aliases={i + 1: i for i in range(len(arrays))},
        compiler_params=pltpu.CompilerParams(vmem_limit_bytes=60 * MIB),
    )(after, *arrays)


def parts_of(size, count):
    step = -(-size // (16 * count)) * 16
    return [slice(i, min(i + step, size)) for i in range(0, size, step)]


def head_kernel(
    text_hbm, feats_hbm, win_hbm, wout_hbm, partial_ref, pre_ref, emb_ref,
    text_ref, feats_ref, win_ref, wout_ref, hidden_ref, sems,
):
    spans = parts_of(win_ref.shape[0], 3)
    copies = [
        pltpu.make_async_copy(text_hbm, text_ref, sems.at[0]),
        pltpu.make_async_copy(feats_hbm, feats_ref, sems.at[1]),
    ]
    copies += [
        pltpu.make_async_copy(win_hbm.at[span], win_ref.at[span], sems.at[3 + i])
        for i, span in enumerate(spans)
    ]
    copies.append(pltpu.make_async_copy(wout_hbm, wout_ref, sems.at[2]))
    for copy in copies:
        copy.start()
    copies[0].wait()
    text = text_ref[...].astype(F32)
    emb_ref[...] = (text * lax.rsqrt(jnp.sum(text * text, axis=-1, keepdims=True) + EPS)).astype(BF)
    copies[1].wait()
    for i, span in enumerate(spans):
        copies[2 + i].wait()
        pre = lax.dot_general(win_ref[span, :], feats_ref[...], NT, preferred_element_type=F32)
        hidden_ref[span, :] = gelu_val(pre, gelu_tanh(pre)).astype(BF)
        pre_ref[span, :] = pre.astype(BF)
    copies[-1].wait()
    partial_ref[...] = lax.dot_general(
        hidden_ref[...], wout_ref[...], (((0,), (0,)), ((), ())), preferred_element_type=F32
    ).astype(BF)


def feats_kernel(where_ref, feats_ref, *out_refs):
    x_index, l_index, c_index = where_ref[0], where_ref[1], where_ref[2]
    rows, width = feats_ref.shape
    h_count = out_refs[0].shape[1] // LANES
    chunk = width // (8 * h_count)
    source = lax.broadcasted_iota(jnp.int32, (2 * LANES, LANES), 0)
    target = lax.broadcasted_iota(jnp.int32, (2 * LANES, LANES), 1)
    inside = (target >= OUT_COLS) & (target < OUT_COLS + chunk)
    for rx, rl, rc in [(a, b, c) for a in range(2) for b in range(2) for c in range(2)]:
        for h in range(h_count):
            place = ((rx ^ x_index) * h_count + h) * 2 + (rl ^ l_index)
            begin = (place * 2 + (rc ^ c_index)) * chunk
            window = jnp.minimum(begin // LANES * LANES, width - 2 * LANES)
            shift = begin - window - OUT_COLS
            move = jnp.where(inside & (source == target + shift), 1.0, 0.0).astype(BF)
            piece = feats_ref[:, pl.ds(pl.multiple_of(window, LANES), 2 * LANES)]
            piece = jnp.dot(piece, move, preferred_element_type=F32).astype(BF)
            out_refs[rx * 2 + rl][rc * rows : (rc + 1) * rows, h * LANES : (h + 1) * LANES] = piece


def unit_kernel(got_ref, unit_ref, inv_ref, spread_ref):
    projected = jnp.sum(got_ref[...].astype(F32), axis=0)
    inv_norm = lax.rsqrt(jnp.sum(projected * projected, axis=-1, keepdims=True) + EPS)
    unit = projected * inv_norm
    unit_ref[...] = unit
    inv_ref[...] = jnp.broadcast_to(inv_norm, inv_ref.shape)
    spread_ref[...] = jnp.broadcast_to(unit.astype(BF)[None], spread_ref.shape)


def expo_block(scale_val, video_ref, text):
    count, own_rows, emb = video_ref.shape
    video = video_ref[...].reshape(count * own_rows, emb)
    return jnp.exp(scale_val * lax.dot_general(video, text, NT, preferred_element_type=F32))


def column_place(where_ref, block):
    return lax.rem(where_ref[4] + block, 4) * 2


def logits_kernel(where_ref, scale_ref, video_ref, *refs):
    text_refs, (spread_ref, col_ref) = refs[:4], refs[4:]
    for block in range(4):
        expo = expo_block(scale_ref[0], video_ref, text_refs[block][...])
        col_part = jnp.sum(expo, axis=0, keepdims=True)
        for half in range(2):
            col_ref[pl.ds(column_place(where_ref, block) + half, 1), :] = col_part[
                :, half * LANES : (half + 1) * LANES
            ]
    spread_ref[...] = jnp.broadcast_to(col_ref[...][None], spread_ref.shape)


def weights_kernel(where_ref, scale_ref, video_ref, *refs):
    text_refs, (got_ref, packed_ref, log_ref, inv_ref) = refs[:4], refs[4:]
    count, own_rows, emb = video_ref.shape
    rows = count * own_rows
    col_sum = jnp.sum(got_ref[...], axis=0)
    log_ref[...] = jnp.log(col_sum)
    inv_ref[...] = 1.0 / col_sum
    first = jnp.zeros((rows, emb), F32)
    second = jnp.zeros((rows, emb), F32)
    row_part = jnp.zeros((rows, 1), F32)
    for block in range(4):
        text = text_refs[block][...]
        expo = expo_block(scale_ref[0], video_ref, text)
        row_part += jnp.sum(expo, axis=1, keepdims=True)
        place = column_place(where_ref, block)
        inv = jnp.concatenate([inv_ref[pl.ds(place + half, 1), :] for half in range(2)], axis=1)
        first += jnp.dot(expo.astype(BF), text, preferred_element_type=F32)
        second += jnp.dot((expo * inv).astype(BF), text, preferred_element_type=F32)
    packed_ref[:, :, :emb] = first.astype(BF).reshape(count, own_rows, emb)
    packed_ref[:, :, emb : 2 * emb] = second.astype(BF).reshape(count, own_rows, emb)
    row_hi = row_part.astype(BF).astype(F32)
    lane = lax.broadcasted_iota(jnp.int32, (rows, LANES), 1)
    both = jnp.where(lane < LANES // 2, row_hi, row_part - row_hi)
    packed_ref[:, :, 2 * emb :] = both.astype(BF).reshape(count, own_rows, LANES)


def proj_kernel(where_ref, scale_ref, back_ref, unit_ref, inv_ref, text_ref, log_ref, out_ref, *, sharers):
    scale_val = scale_ref[0]
    own_rows, emb = unit_ref.shape
    back = jnp.sum(back_ref[...].astype(F32), axis=0)
    half = 2 * emb + LANES // 2
    row_sum = back[:, 2 * emb : 2 * emb + 1] + back[:, half : half + 1]
    weighted = back[:, :emb] / row_sum + back[:, emb : 2 * emb]
    text = text_ref[where_ref[3]].astype(F32)
    unit = unit_ref[...]
    positive = scale_val * jnp.sum(unit.astype(BF).astype(F32) * text, axis=-1, keepdims=True)
    rows_piece = jnp.sum(jnp.log(row_sum) - 2.0 * positive, axis=0, keepdims=True)
    cols_piece = jnp.sum(jnp.sum(log_ref[...], axis=0, keepdims=True), axis=1, keepdims=True)
    a, b, c = split3(rows_piece + cols_piece / sharers)
    grad_emb = 0.5 * scale_val * weighted - scale_val * text
    grad_proj = inv_ref[:, :1] * (
        grad_emb - unit * jnp.sum(unit * grad_emb, axis=-1, keepdims=True)
    )
    lane = lax.broadcasted_iota(jnp.int32, (own_rows, LANES), 1)
    row = lax.broadcasted_iota(jnp.int32, (own_rows, LANES), 0)
    loss = jnp.where(lane == 0, a, jnp.where(lane == 1, b, jnp.where(lane == 2, c, 0.0)))
    loss = jnp.where(row == 0, loss, 0.0)
    sent = jnp.concatenate([grad_proj, loss], axis=1).astype(BF)
    out_ref[...] = jnp.broadcast_to(sent[None], out_ref.shape)


def gelu_kernel(*refs):
    pre_refs, (hidden_ref, der_ref) = refs[:8], refs[8:]
    rows = pre_refs[0].shape[1]
    for block in range(8):
        pre = pre_refs[block][...].astype(F32)
        tanh_val = gelu_tanh(pre)
        span = slice(block * rows, (block + 1) * rows)
        hidden_ref[:, span] = gelu_val(pre, tanh_val).astype(BF)
        der_ref[:, span] = gelu_der(pre, tanh_val).astype(BF)


def grads_kernel(where_ref, own_hbm, other_hbm, wout_hbm, der_hbm, hidden_hbm, *refs):
    feats_hbm, refs = refs[:8], refs[8:]
    out_ref, grads_ref, wout_ref, der_ref, hidden_ref, feats_ref, sems = refs
    x_index, l_index, c_index = where_ref[0], where_ref[1], where_ref[2]
    rows = own_hbm.shape[1]
    emb = wout_ref.shape[1]
    hid = wout_ref.shape[0]
    h_count = out_ref.shape[0]
    copies = []
    for block in range(8):
        rx, rl, rc = block // 4, block // 2 % 2, block % 2
        source = other_hbm if rc else own_hbm
        copies.append((source.at[(rx ^ x_index) * 2 + (rl ^ l_index)], grads_ref.at[block]))
    copies.append((wout_hbm, wout_ref))
    copies.append((der_hbm, der_ref))
    for block in range(8):
        side = block % 2 * rows
        copies.append((feats_hbm[block].at[pl.ds(side, rows)], feats_ref.at[pl.ds(block * rows, rows)]))
    copies.append((hidden_hbm, hidden_ref))
    copies = [pltpu.make_async_copy(a, b, sems.at[i]) for i, (a, b) in enumerate(copies)]
    for copy in copies:
        copy.start()
    source = lax.broadcasted_iota(jnp.int32, (emb, LANES), 0)
    target = lax.broadcasted_iota(jnp.int32, (emb, LANES), 1)
    column = ((target // OUT_COLS) * 2 + l_index) * 2 + c_index
    column = x_index * (emb // 2) + column * OUT_COLS + target % OUT_COLS
    pick = (target < h_count * OUT_COLS) & (source == column)
    pick = jnp.where(pick, 1.0, 0.0).astype(BF)
    for copy in copies[:9]:
        copy.wait()
    grads = grads_ref[:, :, :emb].reshape(8 * rows, emb)
    picked = jnp.dot(grads, pick, preferred_element_type=F32).astype(BF)
    loss = jnp.zeros((1, LANES), F32)
    for block in range(8):
        loss += jnp.sum(grads_ref[block, :, emb:].astype(F32), axis=0, keepdims=True)
    a, b, c = split3(jnp.sum(loss, axis=1, keepdims=True))
    spans = parts_of(hid, 2)
    for i, span in enumerate(spans):
        size = span.stop - span.start
        lane = lax.broadcasted_iota(jnp.int32, (size, LANES), 1)
        grad_hidden = lax.dot_general(wout_ref[span, :], grads, NT, preferred_element_type=F32)
        if i == 0:
            copies[9].wait()
        grad_pre = (grad_hidden * der_ref[span, :].astype(F32)).astype(BF)
        if i == 0:
            for copy in copies[10:]:
                copy.wait()
        total = jnp.dot(grad_pre, feats_ref[...], preferred_element_type=F32)
        outer = jnp.dot(hidden_ref[span, :], picked, preferred_element_type=F32)
        for h in range(h_count):
            moved = outer if h == 0 else pltpu.roll(outer, LANES - h * OUT_COLS, 1)
            value = jnp.where(lane < OUT_COLS, moved, total[:, h * LANES : (h + 1) * LANES])
            if i == 0:
                row = lax.broadcasted_iota(jnp.int32, (size, LANES), 0)
                extra = jnp.where(row == 0, a, jnp.where(row == 1, b, c))
                value = jnp.where((lane == LANES - 1) & (row < 3), extra, value)
            out_ref[h, span, :] = value.astype(BF)


def final_kernel(got_ref, in_ref, out_ref, loss_ref, *, batch_total):
    total = jnp.sum(got_ref[...].astype(F32), axis=0)
    turned = total.T
    in_rows = in_ref.shape[0]
    out_ref[...] = turned[:OUT_COLS]
    in_ref[...] = turned[OUT_COLS : OUT_COLS + in_rows]
    loss = jnp.sum(total[:3, LANES - 1 :], axis=0, keepdims=True) / (2.0 * batch_total)
    loss_ref[...] = loss


def ring(value, step):
    return lax.ppermute(value, "zh", [(i, (i - step) % 4) for i in range(4)])


def on_device(video_feats, text_feats, weight_in, weight_out, logit_scale):
    rows, d_in = video_feats.shape
    hid, emb = weight_out.shape
    mp_count = lax.axis_size(MP)
    h_count = lax.axis_size("zh")
    own_rows = rows // mp_count
    batch_total = rows * lax.axis_size(DP)
    where = [lax.axis_index(name) for name in ("x_lo", "zl", "core", MP, "zh")]
    where = jnp.stack(where).astype(jnp.int32)

    partial_value, pre_bf, text_emb = call(
        head_kernel, [((rows, emb), BF), ((hid, rows), BF), ((rows, emb), BF)], LIM[0],
        text_feats, video_feats, weight_in.T, weight_out, raw=True,
        scratch=[
            pltpu.VMEM((rows, emb), BF), pltpu.VMEM((rows, d_in), BF), pltpu.VMEM((hid, d_in), BF),
            pltpu.VMEM((hid, emb), BF), pltpu.VMEM((hid, rows), BF), pltpu.SemaphoreType.DMA((6,)),
        ],
    )
    got = exchange(partial_value.reshape(mp_count, own_rows, emb), MP)

    texts = [ring(text_emb, step) for step in (1, 2, 3)]
    feats = call(
        feats_kernel, [((2 * rows, h_count * LANES), BF)] * 4, LIM[1], where, video_feats, scalars=1
    )
    unit, inv_norm, video = call(
        unit_kernel,
        [((own_rows, emb), F32), ((own_rows, LANES), F32), ((8, own_rows, emb), BF)],
        LIM[2], got, after=(feats[0],),
    )
    give_l, give_x, give_xl, pre_bf = gate(inv_norm, feats[1], feats[2], feats[3], pre_bf)
    feats_x = swap(give_x, "x_lo")
    feats_l = swap(give_l, "zl")
    feats_xl = swap(swap(give_xl, "x_lo"), "zl")
    pre_l = swap(pre_bf, "zl")
    sides = [pre_bf, pre_l, swap(pre_bf, "x_lo"), swap(pre_l, "x_lo")]
    pre = [value for side in sides for value in (side, swap(side, "core"))]

    video_rows = exchange(video, CUBE)
    (cols,) = call(
        logits_kernel, [((4 * mp_count, 8, LANES), F32)], LIM[3],
        where, logit_scale, video_rows, text_emb, *texts, scalars=2,
        scratch=[pltpu.VMEM((8, LANES), F32)],
    )
    cols = exchange(cols, COLS)
    packed, logs = call(
        weights_kernel, [((8, own_rows, 2 * emb + LANES), BF), ((8, LANES), F32)], LIM[4],
        where, logit_scale, video_rows, text_emb, *texts, cols, scalars=2,
        scratch=[pltpu.VMEM((8, LANES), F32)],
    )
    back = exchange(packed, CUBE)
    (sent,) = call(
        functools.partial(proj_kernel, sharers=4 * mp_count),
        [((4 * mp_count, own_rows, emb + LANES), BF)], LIM[5],
        where, logit_scale, back, unit, inv_norm, text_emb.reshape(mp_count, own_rows, emb), logs,
        scalars=2, after=(feats_x, feats_l, feats_xl, *pre[1:]),
    )
    grads = exchange(sent, SPREAD).reshape(4, rows, emb + LANES)
    other = swap(grads, "core")
    feats_q = [
        value for side in (feats[0], feats_l, feats_x, feats_xl) for value in (side, swap(side, "core"))
    ]
    hidden_all, der_all = call(
        gelu_kernel, [((hid, 8 * rows), BF), ((hid, 8 * rows), BF)], LIM[6], *pre
    )
    (packed,) = call(
        grads_kernel, [((h_count, hid, LANES), BF)], LIM[7],
        where, grads, other, weight_out, der_all, hidden_all, *feats_q, scalars=1, raw=True,
        scratch=[
            pltpu.VMEM((8, rows, emb + LANES), BF), pltpu.VMEM((hid, emb), BF),
            pltpu.VMEM((hid, 8 * rows), BF), pltpu.VMEM((hid, 8 * rows), BF),
            pltpu.VMEM((8 * rows, h_count * LANES), BF), pltpu.SemaphoreType.DMA((19,)),
        ],
    )
    final = exchange(packed, "zh")
    in_rows = d_in // lax.axis_size(DP)
    grad_in, grad_out, loss = call(
        functools.partial(final_kernel, batch_total=batch_total),
        [((in_rows, hid), F32), ((OUT_COLS, hid), F32), ((1, 1), F32)],
        LIM[8], final,
    )
    return (loss.reshape(1), grad_in, grad_out.T)


def solution(mesh):
    fine = Mesh(mesh.devices.reshape(2, 4, 2, 2, mesh.devices.shape[1] // 2, 2), DP + MP)
    in_specs = (P(DP, None), P(DP, None), P(None, MP), P(MP, None), P())
    out_specs = (P(), P(DP, MP), P(MP, DP))
    return jax.shard_map(
        on_device, mesh=fine, in_specs=in_specs, out_specs=out_specs, check_vma=False
    )
```

```python
import functools

import jax
import jax.numpy as jnp
from jax import lax
from jax.experimental import pallas as pl
from jax.experimental.pallas import tpu as pltpu
from jax.sharding import Mesh, PartitionSpec as P

EPS = 1e-06
GELU_C = 0.7978845608
GELU_K = 0.044715
MP = ("y", "x_hi")
DP = ("x_lo", "z", "core")
PLANE = ("x_lo", "core", "y", "x_hi")
SPREAD = ("x_lo", "y", "x_hi")
BF = jnp.bfloat16
F32 = jnp.float32
LANES = 128
OUT_COLS = 16
MIB = 1 << 20
LIM = (60, 60, 8, 8, 8, 60, 60, 60, 16)
NT = (((1,), (1,)), ((), ()))


def gelu_val(values, tanh_val):
    return 0.5 * values * (1.0 + tanh_val)


def gelu_der(values, tanh_val):
    return 0.5 * (1.0 + tanh_val) + 0.5 * values * (1.0 - tanh_val * tanh_val) * GELU_C * (
        1.0 + 3.0 * GELU_K * values * values
    )


def gelu_tanh(values):
    return jnp.tanh(GELU_C * (values + GELU_K * values * values * values))


def swap(value, axis):
    return lax.ppermute(value, axis, [(0, 1), (1, 0)])


def exchange(value, axis):
    return lax.all_to_all(value, axis, 0, 0)


def split3(value):
    first = value.astype(BF).astype(F32)
    second = (value - first).astype(BF).astype(F32)
    return first, second, value - first - second


def call(kernel, outs, vmem, *args, scalars=0, scratch=(), after=(), raw=False):
    held = [] if raw else list(args[scalars:])
    total = len(args) + len(after)

    def body(*refs):
        outputs = refs[total : total + len(outs)]
        rest = refs[total + len(outs) :]
        if raw:
            kernel(*refs[: len(args)], *outputs, *rest)
            return
        places, sems, rest = rest[: len(held)], rest[len(held)], rest[len(held) + 1 :]
        copies = [
            pltpu.make_async_copy(refs[scalars + i], places[i], sems.at[i])
            for i in range(len(held))
        ]
        for copy in copies:
            copy.start()
        for copy in copies:
            copy.wait()
        kernel(*refs[:scalars], *places, *outputs, *rest)

    places = [pltpu.VMEM(a.shape, a.dtype) for a in held]
    if held:
        places.append(pltpu.SemaphoreType.DMA((len(held),)))
    anywhere = pl.BlockSpec(memory_space=pl.ANY)
    return pl.pallas_call(
        body,
        grid=(1,),
        out_shape=[jax.ShapeDtypeStruct(s, d) for s, d in outs],
        in_specs=[pl.BlockSpec(memory_space=pltpu.SMEM)] * scalars + [anywhere] * (total - scalars),
        out_specs=[whole(s) for s, _ in outs],
        scratch_shapes=[*places, *scratch],
        compiler_params=pltpu.CompilerParams(vmem_limit_bytes=vmem * MIB),
        cost_estimate=pl.CostEstimate(flops=1024, bytes_accessed=1024, transcendentals=0),
    )(*args, *after)


def whole(shape):
    return pl.BlockSpec(shape, lambda i: (0,) * len(shape), pipeline_mode=pl.Buffered(1))


def gate(first, *arrays, after=()):
    after = (first, *after)
    anywhere = pl.BlockSpec(memory_space=pl.ANY)
    return pl.pallas_call(
        lambda *refs: None,
        out_shape=[jax.ShapeDtypeStruct(a.shape, a.dtype) for a in arrays],
        in_specs=[anywhere] * (len(arrays) + len(after)),
        out_specs=[anywhere] * len(arrays),
        input_output_aliases={i + len(after): i for i in range(len(arrays))},
        compiler_params=pltpu.CompilerParams(vmem_limit_bytes=60 * MIB),
    )(*after, *arrays)


def parts_of(size, count):
    step = -(-size // (16 * count)) * 16
    return [slice(i, min(i + step, size)) for i in range(0, size, step)]


def head_kernel(
    text_hbm, feats_hbm, win_hbm, wout_hbm, partial_ref, pre_ref, emb_ref,
    text_ref, feats_ref, win_ref, wout_ref, hidden_ref, sems,
):
    spans = parts_of(win_ref.shape[0], 3)
    copies = [
        pltpu.make_async_copy(text_hbm, text_ref, sems.at[0]),
        pltpu.make_async_copy(feats_hbm, feats_ref, sems.at[1]),
    ]
    copies += [
        pltpu.make_async_copy(win_hbm.at[span], win_ref.at[span], sems.at[3 + i])
        for i, span in enumerate(spans)
    ]
    copies.append(pltpu.make_async_copy(wout_hbm, wout_ref, sems.at[2]))
    for copy in copies:
        copy.start()
    copies[0].wait()
    text = text_ref[...].astype(F32)
    emb_ref[...] = (text * lax.rsqrt(jnp.sum(text * text, axis=-1, keepdims=True) + EPS)).astype(BF)
    copies[1].wait()
    for i, span in enumerate(spans):
        copies[2 + i].wait()
        pre = lax.dot_general(win_ref[span, :], feats_ref[...], NT, preferred_element_type=F32)
        hidden_ref[span, :] = gelu_val(pre, gelu_tanh(pre)).astype(BF)
        pre_ref[span, :] = pre.astype(BF)
    copies[-1].wait()
    partial_ref[...] = lax.dot_general(
        hidden_ref[...], wout_ref[...], (((0,), (0,)), ((), ())), preferred_element_type=F32
    ).astype(BF)


def feats_kernel(where_ref, feats_ref, own_ref, give_ref):
    x_index, c_index = where_ref[0], where_ref[1]
    rows, width = feats_ref.shape
    z_count = own_ref.shape[1] // LANES
    chunk = width // (4 * z_count)
    source = lax.broadcasted_iota(jnp.int32, (2 * LANES, LANES), 0)
    target = lax.broadcasted_iota(jnp.int32, (2 * LANES, LANES), 1)
    inside = (target >= OUT_COLS) & (target < OUT_COLS + chunk)
    for rx, rc in [(a, b) for a in range(2) for b in range(2)]:
        for z in range(z_count):
            begin = (((rx ^ x_index) * z_count + z) * 2 + (rc ^ c_index)) * chunk
            window = jnp.minimum(begin // LANES * LANES, width - 2 * LANES)
            shift = begin - window - OUT_COLS
            move = jnp.where(inside & (source == target + shift), 1.0, 0.0).astype(BF)
            piece = feats_ref[:, pl.ds(pl.multiple_of(window, LANES), 2 * LANES)]
            piece = jnp.dot(piece, move, preferred_element_type=F32).astype(BF)
            out_ref = (own_ref, give_ref)[rx]
            out_ref[rc * rows : (rc + 1) * rows, z * LANES : (z + 1) * LANES] = piece


def unit_kernel(got_ref, unit_ref, inv_ref, spread_ref):
    projected = jnp.sum(got_ref[...].astype(F32), axis=0)
    inv_norm = lax.rsqrt(jnp.sum(projected * projected, axis=-1, keepdims=True) + EPS)
    unit = projected * inv_norm
    unit_ref[...] = unit
    inv_ref[...] = jnp.broadcast_to(inv_norm, inv_ref.shape)
    spread_ref[...] = jnp.broadcast_to(unit.astype(BF)[None], spread_ref.shape)


def expo_block(scale_val, video_ref, text):
    count, own_rows, emb = video_ref.shape
    video = video_ref[...].reshape(count * own_rows, emb)
    return jnp.exp(scale_val * lax.dot_general(video, text, NT, preferred_element_type=F32))


def column_place(where_ref, block):
    return (((block // 2) ^ where_ref[0]) * 2 + ((block % 2) ^ where_ref[1])) * 2


def logits_kernel(where_ref, scale_ref, video_ref, *refs):
    text_refs, (spread_ref, col_ref) = refs[:4], refs[4:]
    for block in range(4):
        expo = expo_block(scale_ref[0], video_ref, text_refs[block][...])
        col_part = jnp.sum(expo, axis=0, keepdims=True)
        for half in range(2):
            col_ref[pl.ds(column_place(where_ref, block) + half, 1), :] = col_part[
                :, half * LANES : (half + 1) * LANES
            ]
    spread_ref[...] = jnp.broadcast_to(col_ref[...][None], spread_ref.shape)


def weights_kernel(where_ref, scale_ref, video_ref, *refs):
    text_refs, (got_ref, packed_ref, log_ref, inv_ref) = refs[:4], refs[4:]
    count, own_rows, emb = video_ref.shape
    rows = count * own_rows
    col_sum = jnp.sum(got_ref[...], axis=0)
    log_ref[...] = jnp.log(col_sum)
    inv_ref[...] = 1.0 / col_sum
    first = jnp.zeros((rows, emb), F32)
    second = jnp.zeros((rows, emb), F32)
    row_part = jnp.zeros((rows, 1), F32)
    for block in range(4):
        text = text_refs[block][...]
        expo = expo_block(scale_ref[0], video_ref, text)
        row_part += jnp.sum(expo, axis=1, keepdims=True)
        place = column_place(where_ref, block)
        inv = jnp.concatenate([inv_ref[pl.ds(place + half, 1), :] for half in range(2)], axis=1)
        first += jnp.dot(expo.astype(BF), text, preferred_element_type=F32)
        second += jnp.dot((expo * inv).astype(BF), text, preferred_element_type=F32)
    packed_ref[:, :, :emb] = first.astype(BF).reshape(count, own_rows, emb)
    packed_ref[:, :, emb : 2 * emb] = second.astype(BF).reshape(count, own_rows, emb)
    row_hi = row_part.astype(BF).astype(F32)
    lane = lax.broadcasted_iota(jnp.int32, (rows, LANES), 1)
    both = jnp.where(lane < LANES // 2, row_hi, row_part - row_hi)
    packed_ref[:, :, 2 * emb :] = both.astype(BF).reshape(count, own_rows, LANES)


def proj_kernel(where_ref, scale_ref, back_ref, unit_ref, inv_ref, text_ref, log_ref, out_ref, *, sharers):
    scale_val = scale_ref[0]
    own_rows, emb = unit_ref.shape
    back = jnp.sum(back_ref[...].astype(F32), axis=0)
    half = 2 * emb + LANES // 2
    row_sum = back[:, 2 * emb : 2 * emb + 1] + back[:, half : half + 1]
    weighted = back[:, :emb] / row_sum + back[:, emb : 2 * emb]
    text = text_ref[where_ref[2]].astype(F32)
    unit = unit_ref[...]
    positive = scale_val * jnp.sum(unit.astype(BF).astype(F32) * text, axis=-1, keepdims=True)
    rows_piece = jnp.sum(jnp.log(row_sum) - 2.0 * positive, axis=0, keepdims=True)
    cols_piece = jnp.sum(jnp.sum(log_ref[...], axis=0, keepdims=True), axis=1, keepdims=True)
    a, b, c = split3(rows_piece + cols_piece / sharers)
    grad_emb = 0.5 * scale_val * weighted - scale_val * text
    grad_proj = inv_ref[:, :1] * (
        grad_emb - unit * jnp.sum(unit * grad_emb, axis=-1, keepdims=True)
    )
    lane = lax.broadcasted_iota(jnp.int32, (own_rows, LANES), 1)
    row = lax.broadcasted_iota(jnp.int32, (own_rows, LANES), 0)
    loss = jnp.where(lane == 0, a, jnp.where(lane == 1, b, jnp.where(lane == 2, c, 0.0)))
    loss = jnp.where(row == 0, loss, 0.0)
    sent = jnp.concatenate([grad_proj, loss], axis=1).astype(BF)
    out_ref[...] = jnp.broadcast_to(sent[None], out_ref.shape)


def gelu_kernel(*refs):
    pre_refs, (hidden_ref, der_ref) = refs[:4], refs[4:]
    rows = pre_refs[0].shape[1]
    for block in range(4):
        pre = pre_refs[block][...].astype(F32)
        tanh_val = gelu_tanh(pre)
        span = slice(block * rows, (block + 1) * rows)
        hidden_ref[:, span] = gelu_val(pre, tanh_val).astype(BF)
        der_ref[:, span] = gelu_der(pre, tanh_val).astype(BF)


def grads_kernel(where_ref, own_hbm, other_hbm, wout_hbm, hidden_hbm, der_hbm, *refs):
    feats_hbm, refs = refs[:4], refs[4:]
    out_ref, grads_ref, wout_ref, der_ref, hidden_ref, feats_ref, sems = refs
    x_index, c_index = where_ref[0], where_ref[1]
    rows = own_hbm.shape[1]
    hid, emb = wout_ref.shape
    z_count = out_ref.shape[0]
    spans = parts_of(hid, 2)
    copies = []
    for block in range(4):
        rx, rc = block // 2, block % 2
        source = other_hbm if rc else own_hbm
        copies.append((source.at[rx ^ x_index], grads_ref.at[block]))
    copies.append((wout_hbm, wout_ref))
    copies.append((der_hbm.at[spans[0]], der_ref.at[spans[0]]))
    for block in range(4):
        side = pl.ds(block % 2 * rows, rows)
        copies.append((feats_hbm[block].at[side], feats_ref.at[pl.ds(block * rows, rows)]))
    copies.append((hidden_hbm.at[spans[0]], hidden_ref.at[spans[0]]))
    copies.append((der_hbm.at[spans[1]], der_ref.at[spans[1]]))
    copies.append((hidden_hbm.at[spans[1]], hidden_ref.at[spans[1]]))
    copies = [pltpu.make_async_copy(a, b, sems.at[i]) for i, (a, b) in enumerate(copies)]
    for copy in copies:
        copy.start()
    source = lax.broadcasted_iota(jnp.int32, (emb, LANES), 0)
    target = lax.broadcasted_iota(jnp.int32, (emb, LANES), 1)
    column = (target // OUT_COLS) * 2 + c_index
    column = x_index * (emb // 2) + column * OUT_COLS + target % OUT_COLS
    pick = jnp.where(source == column, 1.0, 0.0).astype(BF)
    for copy in copies[:5]:
        copy.wait()
    grads = grads_ref[:, :, :emb].reshape(4 * rows, emb)
    picked = jnp.dot(grads, pick, preferred_element_type=F32).astype(BF)
    loss = jnp.zeros((1, LANES), F32)
    for block in range(4):
        loss += jnp.sum(grads_ref[block, :, emb:].astype(F32), axis=0, keepdims=True)
    a, b, c = split3(jnp.sum(loss, axis=1, keepdims=True))
    for i, span in enumerate(spans):
        size = span.stop - span.start
        lane = lax.broadcasted_iota(jnp.int32, (size, LANES), 1)
        grad_hidden = lax.dot_general(wout_ref[span, :], grads, NT, preferred_element_type=F32)
        copies[(5, 11)[i]].wait()
        grad_pre = (grad_hidden * der_ref[span, :].astype(F32)).astype(BF)
        if i == 0:
            for copy in copies[6:10]:
                copy.wait()
        total = jnp.dot(grad_pre, feats_ref[...], preferred_element_type=F32)
        copies[(10, 12)[i]].wait()
        outer = jnp.dot(hidden_ref[span, :], picked, preferred_element_type=F32)
        for z in range(z_count):
            moved = outer if z == 0 else pltpu.roll(outer, LANES - z * OUT_COLS, 1)
            value = jnp.where(lane < OUT_COLS, moved, total[:, z * LANES : (z + 1) * LANES])
            if i == 0:
                row = lax.broadcasted_iota(jnp.int32, (size, LANES), 0)
                extra = jnp.where(row == 0, a, jnp.where(row == 1, b, c))
                value = jnp.where((lane == LANES - 1) & (row < 3), extra, value)
            out_ref[z, span, :] = value.astype(BF)


def final_kernel(got_ref, in_ref, out_ref, loss_ref, *, batch_total):
    total = jnp.sum(got_ref[...].astype(F32), axis=0)
    turned = total.T
    in_rows = in_ref.shape[0]
    out_ref[...] = turned[:OUT_COLS]
    in_ref[...] = turned[OUT_COLS : OUT_COLS + in_rows]
    loss = jnp.sum(total[:3, LANES - 1 :], axis=0, keepdims=True) / (2.0 * batch_total)
    loss_ref[...] = loss


def on_device(video_feats, text_feats, weight_in, weight_out, logit_scale):
    rows, d_in = video_feats.shape
    hid, emb = weight_out.shape
    mp_count = lax.axis_size(MP)
    own_rows = rows // mp_count
    batch_total = rows * lax.axis_size(DP)
    where = [lax.axis_index(name) for name in ("x_lo", "core", MP)]
    where = jnp.stack(where).astype(jnp.int32)

    partial_value, pre_bf, text_emb = call(
        head_kernel, [((rows, emb), BF), ((hid, rows), BF), ((rows, emb), BF)], LIM[0],
        text_feats, video_feats, weight_in.T, weight_out, raw=True,
        scratch=[
            pltpu.VMEM((rows, emb), BF), pltpu.VMEM((rows, d_in), BF), pltpu.VMEM((hid, d_in), BF),
            pltpu.VMEM((hid, emb), BF), pltpu.VMEM((hid, rows), BF), pltpu.SemaphoreType.DMA((6,)),
        ],
    )
    got = exchange(partial_value.reshape(mp_count, own_rows, emb), MP)

    text_x = swap(text_emb, "x_lo")
    texts = [swap(text_emb, "core"), text_x, swap(text_x, "core")]
    z_count = lax.axis_size("z")
    feats, give_x = call(
        feats_kernel, [((2 * rows, z_count * LANES), BF)] * 2, LIM[1], where, video_feats, scalars=1
    )
    unit, inv_norm, video = call(
        unit_kernel,
        [((own_rows, emb), F32), ((own_rows, LANES), F32), ((8, own_rows, emb), BF)],
        LIM[2], got, after=(feats, text_x),
    )
    give_x, pre_own = gate(inv_norm, give_x, pre_bf)
    feats_x = swap(give_x, "x_lo")

    video_rows = exchange(video, "z")
    (cols,) = call(
        logits_kernel, [((4 * mp_count, 8, LANES), F32)], LIM[3],
        where, logit_scale, video_rows, text_emb, *texts, scalars=2,
        scratch=[pltpu.VMEM((8, LANES), F32)],
    )
    cols = exchange(cols, PLANE)
    pre_x = swap(pre_own, "x_lo")
    pre = (pre_own, swap(pre_own, "core"), pre_x, swap(pre_x, "core"))
    packed, logs = call(
        weights_kernel, [((8, own_rows, 2 * emb + LANES), BF), ((8, LANES), F32)], LIM[4],
        where, logit_scale, video_rows, text_emb, *texts, cols, scalars=2,
        scratch=[pltpu.VMEM((8, LANES), F32)],
    )
    feats_q = (feats, swap(feats, "core"), feats_x, swap(feats_x, "core"))
    back = exchange(packed, "z")
    (sent,) = call(
        functools.partial(proj_kernel, sharers=4 * mp_count),
        [((2 * mp_count, own_rows, emb + LANES), BF)], LIM[5],
        where, logit_scale, back, unit, inv_norm, text_emb.reshape(mp_count, own_rows, emb), logs,
        scalars=2, after=(feats_q[1], feats_q[3], pre[1], pre[3]),
    )
    gelus = call(gelu_kernel, [((hid, 4 * rows), BF)] * 2, LIM[6], *pre, after=(sent,))
    grads = exchange(sent, SPREAD).reshape(2, rows, emb + LANES)
    (grads,) = gate(gelus[0], grads, after=(gelus[1],))
    other = swap(grads, "core")
    (packed,) = call(
        grads_kernel, [((z_count, hid, LANES), BF)], LIM[7],
        where, grads, other, weight_out, *gelus, *feats_q, scalars=1, raw=True,
        scratch=[
            pltpu.VMEM((4, rows, emb + LANES), BF), pltpu.VMEM((hid, emb), BF),
            pltpu.VMEM((hid, 4 * rows), BF), pltpu.VMEM((hid, 4 * rows), BF),
            pltpu.VMEM((4 * rows, z_count * LANES), BF), pltpu.SemaphoreType.DMA((13,)),
        ],
    )
    final = exchange(packed, "z")
    in_rows = d_in // lax.axis_size(DP)
    grad_in, grad_out, loss = call(
        functools.partial(final_kernel, batch_total=batch_total),
        [((in_rows, hid), F32), ((OUT_COLS, hid), F32), ((1, 1), F32)],
        LIM[8], final,
    )
    return (loss.reshape(1), grad_in, grad_out.T)


def solution(mesh):
    fine = Mesh(mesh.devices.reshape(2, -1, 2, mesh.devices.shape[1] // 2, 2), DP + MP)
    in_specs = (P(DP, None), P(DP, None), P(None, MP), P(MP, None), P())
    out_specs = (P(), P(DP, MP), P(MP, DP))
    return jax.shard_map(
        on_device, mesh=fine, in_specs=in_specs, out_specs=out_specs, check_vma=False
    )
```

```python
import functools

import jax
import jax.numpy as jnp
from jax import lax
from jax.experimental import pallas as pl
from jax.experimental.pallas import tpu as pltpu
from jax.sharding import Mesh, PartitionSpec as P

EPS = 1e-06
GELU_C = 0.7978845608
GELU_K = 0.044715
MP = ("y", "x_hi")
DP = ("x_lo", "z", "core")
PLANE = ("x_lo", "core", "y", "x_hi")
SPREAD = ("x_lo", "y", "x_hi")
BF = jnp.bfloat16
F32 = jnp.float32
LANES = 128
OUT_COLS = 16
FAR = 4
MIB = 1 << 20
LIM = (60, 60, 60, 8, 8, 60, 60, 60, 16, 16)
NT = (((1,), (1,)), ((), ()))


def gelu_val(values, tanh_val):
    return 0.5 * values * (1.0 + tanh_val)


def gelu_der(values, tanh_val):
    return 0.5 * (1.0 + tanh_val) + 0.5 * values * (1.0 - tanh_val * tanh_val) * GELU_C * (
        1.0 + 3.0 * GELU_K * values * values
    )


def gelu_tanh(values):
    return jnp.tanh(GELU_C * (values + GELU_K * values * values * values))


def swap(value, axis):
    return lax.ppermute(value, axis, [(0, 1), (1, 0)])


def exchange(value, axis):
    return lax.all_to_all(value, axis, 0, 0)


def split3(value):
    first = value.astype(BF).astype(F32)
    second = (value - first).astype(BF).astype(F32)
    return first, second, value - first - second


def call(kernel, outs, vmem, *args, scalars=0, scratch=(), after=(), raw=False):
    held = [] if raw else list(args[scalars:])
    total = len(args) + len(after)

    def body(*refs):
        outputs = refs[total : total + len(outs)]
        rest = refs[total + len(outs) :]
        if raw:
            kernel(*refs[: len(args)], *outputs, *rest)
            return
        places, sems, rest = rest[: len(held)], rest[len(held)], rest[len(held) + 1 :]
        copies = [
            pltpu.make_async_copy(refs[scalars + i], places[i], sems.at[i])
            for i in range(len(held))
        ]
        for copy in copies:
            copy.start()
        for copy in copies:
            copy.wait()
        kernel(*refs[:scalars], *places, *outputs, *rest)

    places = [pltpu.VMEM(a.shape, a.dtype) for a in held]
    if held:
        places.append(pltpu.SemaphoreType.DMA((len(held),)))
    anywhere = pl.BlockSpec(memory_space=pl.ANY)
    return pl.pallas_call(
        body,
        grid=(1,),
        out_shape=[jax.ShapeDtypeStruct(s, d) for s, d in outs],
        in_specs=[pl.BlockSpec(memory_space=pltpu.SMEM)] * scalars + [anywhere] * (total - scalars),
        out_specs=[whole(s) for s, _ in outs],
        scratch_shapes=[*places, *scratch],
        compiler_params=pltpu.CompilerParams(vmem_limit_bytes=vmem * MIB),
        cost_estimate=pl.CostEstimate(flops=1024, bytes_accessed=1024, transcendentals=0),
    )(*args, *after)


def whole(shape):
    return pl.BlockSpec(shape, lambda i: (0,) * len(shape), pipeline_mode=pl.Buffered(1))


def gate(first, *arrays, after=()):
    after = (first, *after)
    anywhere = pl.BlockSpec(memory_space=pl.ANY)
    return pl.pallas_call(
        lambda *refs: None,
        out_shape=[jax.ShapeDtypeStruct(a.shape, a.dtype) for a in arrays],
        in_specs=[anywhere] * (len(arrays) + len(after)),
        out_specs=[anywhere] * len(arrays),
        input_output_aliases={i + len(after): i for i in range(len(arrays))},
        compiler_params=pltpu.CompilerParams(vmem_limit_bytes=60 * MIB),
    )(*after, *arrays)


def parts_of(size, count):
    step = -(-size // (16 * count)) * 16
    return [slice(i, min(i + step, size)) for i in range(0, size, step)]


def head_kernel(
    text_hbm, feats_hbm, win_hbm, wout_hbm, partial_ref, pre_ref, emb_ref,
    text_ref, feats_ref, win_ref, wout_ref, hidden_ref, sems,
):
    spans = parts_of(win_ref.shape[0], 3)
    copies = [
        pltpu.make_async_copy(text_hbm, text_ref, sems.at[0]),
        pltpu.make_async_copy(feats_hbm, feats_ref, sems.at[1]),
    ]
    copies += [
        pltpu.make_async_copy(win_hbm.at[span], win_ref.at[span], sems.at[3 + i])
        for i, span in enumerate(spans)
    ]
    copies.append(pltpu.make_async_copy(wout_hbm, wout_ref, sems.at[2]))
    for copy in copies:
        copy.start()
    copies[0].wait()
    text = text_ref[...].astype(F32)
    emb_ref[...] = (text * lax.rsqrt(jnp.sum(text * text, axis=-1, keepdims=True) + EPS)).astype(BF)
    copies[1].wait()
    for i, span in enumerate(spans):
        copies[2 + i].wait()
        pre = lax.dot_general(win_ref[span, :], feats_ref[...], NT, preferred_element_type=F32)
        hidden_ref[span, :] = gelu_val(pre, gelu_tanh(pre)).astype(BF)
        pre_ref[span, :] = pre.astype(BF)
    copies[-1].wait()
    partial_ref[...] = lax.dot_general(
        hidden_ref[...], wout_ref[...], (((0,), (0,)), ((), ())), preferred_element_type=F32
    ).astype(BF)


def feats_kernel(where_ref, feats_ref, own_ref, give_ref):
    x_index, c_index = where_ref[0], where_ref[1]
    rows, width = feats_ref.shape
    z_count = own_ref.shape[1] // LANES
    chunk = width // (4 * z_count)
    source = lax.broadcasted_iota(jnp.int32, (2 * LANES, LANES), 0)
    target = lax.broadcasted_iota(jnp.int32, (2 * LANES, LANES), 1)
    inside = (target >= OUT_COLS) & (target < OUT_COLS + chunk)
    for rx, rc in [(a, b) for a in range(2) for b in range(2)]:
        for z in range(z_count):
            target_z = lax.rem(where_ref[3] + z, z_count)
            begin = (((rx ^ x_index) * z_count + target_z) * 2 + (rc ^ c_index)) * chunk
            window = jnp.minimum(begin // LANES * LANES, width - 2 * LANES)
            shift = begin - window - OUT_COLS
            move = jnp.where(inside & (source == target + shift), 1.0, 0.0).astype(BF)
            piece = feats_ref[:, pl.ds(pl.multiple_of(window, LANES), 2 * LANES)]
            piece = jnp.dot(piece, move, preferred_element_type=F32).astype(BF)
            out_ref = (own_ref, give_ref)[rx]
            out_ref[rc * rows : (rc + 1) * rows, z * LANES : (z + 1) * LANES] = piece


def unit_kernel(got_ref, unit_ref, inv_ref, spread_ref):
    projected = jnp.sum(got_ref[...].astype(F32), axis=0)
    inv_norm = lax.rsqrt(jnp.sum(projected * projected, axis=-1, keepdims=True) + EPS)
    unit = projected * inv_norm
    unit_ref[...] = unit
    inv_ref[...] = jnp.broadcast_to(inv_norm, inv_ref.shape)
    spread_ref[...] = jnp.broadcast_to(unit.astype(BF)[None], spread_ref.shape)


def expo_block(scale_val, video_ref, text):
    count, own_rows, emb = video_ref.shape
    video = video_ref[...].reshape(count * own_rows, emb)
    return jnp.exp(scale_val * lax.dot_general(video, text, NT, preferred_element_type=F32))


def column_place(where_ref, block):
    return (((block // 2) ^ where_ref[0]) * 2 + ((block % 2) ^ where_ref[1])) * 2


def logits_kernel(where_ref, scale_ref, video_ref, *refs):
    text_refs, (spread_ref, col_ref) = refs[:4], refs[4:]
    for block in range(4):
        expo = expo_block(scale_ref[0], video_ref, text_refs[block][...])
        col_part = jnp.sum(expo, axis=0, keepdims=True)
        for half in range(2):
            col_ref[pl.ds(column_place(where_ref, block) + half, 1), :] = col_part[
                :, half * LANES : (half + 1) * LANES
            ]
    spread_ref[...] = jnp.broadcast_to(col_ref[...][None], spread_ref.shape)


def weights_kernel(where_ref, scale_ref, video_ref, *refs):
    text_refs, (got_ref, packed_ref, log_ref, inv_ref) = refs[:4], refs[4:]
    count, own_rows, emb = video_ref.shape
    rows = count * own_rows
    col_sum = jnp.sum(got_ref[...], axis=0)
    log_ref[...] = jnp.log(col_sum)
    inv_ref[...] = 1.0 / col_sum
    first = jnp.zeros((rows, emb), F32)
    second = jnp.zeros((rows, emb), F32)
    row_part = jnp.zeros((rows, 1), F32)
    for block in range(4):
        text = text_refs[block][...]
        expo = expo_block(scale_ref[0], video_ref, text)
        row_part += jnp.sum(expo, axis=1, keepdims=True)
        place = column_place(where_ref, block)
        inv = jnp.concatenate([inv_ref[pl.ds(place + half, 1), :] for half in range(2)], axis=1)
        first += jnp.dot(expo.astype(BF), text, preferred_element_type=F32)
        second += jnp.dot((expo * inv).astype(BF), text, preferred_element_type=F32)
    packed_ref[:, :, :emb] = first.astype(BF).reshape(count, own_rows, emb)
    packed_ref[:, :, emb : 2 * emb] = second.astype(BF).reshape(count, own_rows, emb)
    row_hi = row_part.astype(BF).astype(F32)
    lane = lax.broadcasted_iota(jnp.int32, (rows, LANES), 1)
    both = jnp.where(lane < LANES // 2, row_hi, row_part - row_hi)
    packed_ref[:, :, 2 * emb :] = both.astype(BF).reshape(count, own_rows, LANES)


def proj_kernel(where_ref, scale_ref, back_ref, unit_ref, inv_ref, text_ref, log_ref, out_ref, *, sharers):
    scale_val = scale_ref[0]
    own_rows, emb = unit_ref.shape
    back = jnp.sum(back_ref[...].astype(F32), axis=0)
    half = 2 * emb + LANES // 2
    row_sum = back[:, 2 * emb : 2 * emb + 1] + back[:, half : half + 1]
    weighted = back[:, :emb] / row_sum + back[:, emb : 2 * emb]
    text = text_ref[where_ref[2]].astype(F32)
    unit = unit_ref[...]
    positive = scale_val * jnp.sum(unit.astype(BF).astype(F32) * text, axis=-1, keepdims=True)
    rows_piece = jnp.sum(jnp.log(row_sum) - 2.0 * positive, axis=0, keepdims=True)
    cols_piece = jnp.sum(jnp.sum(log_ref[...], axis=0, keepdims=True), axis=1, keepdims=True)
    a, b, c = split3(rows_piece + cols_piece / sharers)
    grad_emb = 0.5 * scale_val * weighted - scale_val * text
    grad_proj = inv_ref[:, :1] * (
        grad_emb - unit * jnp.sum(unit * grad_emb, axis=-1, keepdims=True)
    )
    lane = lax.broadcasted_iota(jnp.int32, (own_rows, LANES), 1)
    row = lax.broadcasted_iota(jnp.int32, (own_rows, LANES), 0)
    loss = jnp.where(lane == 0, a, jnp.where(lane == 1, b, jnp.where(lane == 2, c, 0.0)))
    loss = jnp.where(row == 0, loss, 0.0)
    sent = jnp.concatenate([grad_proj, loss], axis=1).astype(BF)
    out_ref[...] = jnp.broadcast_to(sent[None], out_ref.shape)


def gelu_kernel(*refs):
    pre_refs, (hidden_ref, der_ref) = refs[:4], refs[4:]
    rows = pre_refs[0].shape[1]
    for block in range(4):
        pre = pre_refs[block][...].astype(F32)
        tanh_val = gelu_tanh(pre)
        span = slice(block * rows, (block + 1) * rows)
        hidden_ref[:, span] = gelu_val(pre, tanh_val).astype(BF)
        der_ref[:, span] = gelu_der(pre, tanh_val).astype(BF)


def grads_kernel(where_ref, own_hbm, other_hbm, wout_hbm, hidden_hbm, der_hbm, *refs):
    feats_hbm, out_refs, refs = refs[:4], refs[4:13], refs[13:]
    grads_ref, wout_ref, der_ref, hidden_ref, feats_ref, sems = refs
    x_index, c_index = where_ref[0], where_ref[1]
    rows = own_hbm.shape[1]
    hid, emb = wout_ref.shape
    z_count = feats_ref.shape[1] // LANES
    spans = parts_of(hid, 2)
    copies = []
    for block in range(4):
        rx, rc = block // 2, block % 2
        source = other_hbm if rc else own_hbm
        copies.append((source.at[rx ^ x_index], grads_ref.at[block]))
    copies.append((wout_hbm, wout_ref))
    copies.append((der_hbm.at[spans[0]], der_ref.at[spans[0]]))
    for block in range(4):
        side = pl.ds(block % 2 * rows, rows)
        copies.append((feats_hbm[block].at[side], feats_ref.at[pl.ds(block * rows, rows)]))
    copies.append((hidden_hbm.at[spans[0]], hidden_ref.at[spans[0]]))
    copies.append((der_hbm.at[spans[1]], der_ref.at[spans[1]]))
    copies.append((hidden_hbm.at[spans[1]], hidden_ref.at[spans[1]]))
    copies = [pltpu.make_async_copy(a, b, sems.at[i]) for i, (a, b) in enumerate(copies)]
    for copy in copies:
        copy.start()
    source = lax.broadcasted_iota(jnp.int32, (emb, LANES), 0)
    target = lax.broadcasted_iota(jnp.int32, (emb, LANES), 1)
    column = lax.rem(where_ref[3] + target // OUT_COLS, z_count) * 2 + c_index
    column = x_index * (emb // 2) + column * OUT_COLS + target % OUT_COLS
    pick = jnp.where(source == column, 1.0, 0.0).astype(BF)
    for copy in copies[:5]:
        copy.wait()
    grads = grads_ref[:, :, :emb].reshape(4 * rows, emb)
    picked = jnp.dot(grads, pick, preferred_element_type=F32).astype(BF)
    loss = jnp.zeros((1, LANES), F32)
    for block in range(4):
        loss += jnp.sum(grads_ref[block, :, emb:].astype(F32), axis=0, keepdims=True)
    a, b, c = split3(jnp.sum(loss, axis=1, keepdims=True))
    for i, span in enumerate(spans):
        size = span.stop - span.start
        lane = lax.broadcasted_iota(jnp.int32, (size, LANES), 1)
        grad_hidden = lax.dot_general(wout_ref[span, :], grads, NT, preferred_element_type=F32)
        copies[(5, 11)[i]].wait()
        grad_pre = (grad_hidden * der_ref[span, :].astype(F32)).astype(BF)
        if i == 0:
            for copy in copies[6:10]:
                copy.wait()
        total = jnp.dot(grad_pre, feats_ref[...], preferred_element_type=F32)
        copies[(10, 12)[i]].wait()
        outer = jnp.dot(hidden_ref[span, :], picked, preferred_element_type=F32)
        for z in range(z_count):
            moved = outer if z == 0 else pltpu.roll(outer, LANES - z * OUT_COLS, 1)
            value = jnp.where(lane < OUT_COLS, moved, total[:, z * LANES : (z + 1) * LANES])
            if i == 0:
                row = lax.broadcasted_iota(jnp.int32, (size, LANES), 0)
                extra = jnp.where(row == 0, a, jnp.where(row == 1, b, c))
                value = jnp.where((lane == LANES - 1) & (row < 3), extra, value)
            if z == FAR:
                out_refs[FAR + 4 * i][...] = value.astype(BF)
            else:
                out_refs[z][span, :] = value.astype(BF)


def near_kernel(up_ref, down_ref, up_far_ref, down_far_ref, up_out, down_out):
    first = up_far_ref.shape[0]
    up_out[:first] = (up_ref[:first].astype(F32) + up_far_ref[...].astype(F32)).astype(BF)
    up_out[first:] = up_ref[first:]
    down_out[:first] = down_ref[:first]
    down_out[first:] = (down_ref[first:].astype(F32) + down_far_ref[...].astype(F32)).astype(BF)


def final_kernel(*refs, batch_total):
    got, (in_ref, out_ref, loss_ref) = refs[:7], refs[7:]
    total = got[0][...].astype(F32)
    for ref in got[1:]:
        total += ref[...].astype(F32)
    turned = total.T
    in_rows = in_ref.shape[0]
    out_ref[...] = turned[:OUT_COLS]
    in_ref[...] = turned[OUT_COLS : OUT_COLS + in_rows]
    loss = jnp.sum(total[:3, LANES - 1 :], axis=0, keepdims=True) / (2.0 * batch_total)
    loss_ref[...] = loss


def ahead(value, step):
    return lax.ppermute(value, "z", [(i, (i + step) % 8) for i in range(8)])


def on_device(video_feats, text_feats, weight_in, weight_out, logit_scale):
    rows, d_in = video_feats.shape
    hid, emb = weight_out.shape
    mp_count = lax.axis_size(MP)
    own_rows = rows // mp_count
    batch_total = rows * lax.axis_size(DP)
    where = [lax.axis_index(name) for name in ("x_lo", "core", MP, "z")]
    where = jnp.stack(where).astype(jnp.int32)

    partial_value, pre_bf, text_emb = call(
        head_kernel, [((rows, emb), BF), ((hid, rows), BF), ((rows, emb), BF)], LIM[0],
        text_feats, video_feats, weight_in.T, weight_out, raw=True,
        scratch=[
            pltpu.VMEM((rows, emb), BF), pltpu.VMEM((rows, d_in), BF), pltpu.VMEM((hid, d_in), BF),
            pltpu.VMEM((hid, emb), BF), pltpu.VMEM((hid, rows), BF), pltpu.SemaphoreType.DMA((6,)),
        ],
    )
    got = exchange(partial_value.reshape(mp_count, own_rows, emb), MP)

    text_x = swap(text_emb, "x_lo")
    texts = [swap(text_emb, "core"), text_x, swap(text_x, "core")]
    z_count = lax.axis_size("z")
    feats, give_x = call(
        feats_kernel, [((2 * rows, z_count * LANES), BF)] * 2, LIM[1], where, video_feats, scalars=1
    )
    unit, inv_norm, video = call(
        unit_kernel,
        [((own_rows, emb), F32), ((own_rows, LANES), F32), ((8, own_rows, emb), BF)],
        LIM[2], got, after=(feats, text_x),
    )
    give_x, pre_own = gate(inv_norm, give_x, pre_bf)
    feats_x = swap(give_x, "x_lo")

    video_rows = exchange(video, "z")
    (cols,) = call(
        logits_kernel, [((4 * mp_count, 8, LANES), F32)], LIM[3],
        where, logit_scale, video_rows, text_emb, *texts, scalars=2,
        scratch=[pltpu.VMEM((8, LANES), F32)],
    )
    cols = exchange(cols, PLANE)
    pre_x = swap(pre_own, "x_lo")
    pre = (pre_own, swap(pre_own, "core"), pre_x, swap(pre_x, "core"))
    packed, logs = call(
        weights_kernel, [((8, own_rows, 2 * emb + LANES), BF), ((8, LANES), F32)], LIM[4],
        where, logit_scale, video_rows, text_emb, *texts, cols, scalars=2,
        scratch=[pltpu.VMEM((8, LANES), F32)],
    )
    feats_q = (feats, swap(feats, "core"), feats_x, swap(feats_x, "core"))
    back = exchange(packed, "z")
    (sent,) = call(
        functools.partial(proj_kernel, sharers=4 * mp_count),
        [((2 * mp_count, own_rows, emb + LANES), BF)], LIM[5],
        where, logit_scale, back, unit, inv_norm, text_emb.reshape(mp_count, own_rows, emb), logs,
        scalars=2, after=(feats_q[1], feats_q[3], pre[1], pre[3]),
    )
    gelus = call(gelu_kernel, [((hid, 4 * rows), BF)] * 2, LIM[6], *pre, after=(sent,))
    grads = exchange(sent, SPREAD).reshape(2, rows, emb + LANES)
    (grads,) = gate(gelus[0], grads, after=(gelus[1],))
    other = swap(grads, "core")
    first = parts_of(hid, 2)[0].stop
    sizes = [hid] * FAR + [first] + [hid] * (7 - FAR) + [hid - first]
    pieces = call(
        grads_kernel, [((size, LANES), BF) for size in sizes], LIM[7],
        where, grads, other, weight_out, *gelus, *feats_q, scalars=1, raw=True,
        scratch=[
            pltpu.VMEM((4, rows, emb + LANES), BF), pltpu.VMEM((hid, emb), BF),
            pltpu.VMEM((hid, 4 * rows), BF), pltpu.VMEM((hid, 4 * rows), BF),
            pltpu.VMEM((4 * rows, z_count * LANES), BF), pltpu.SemaphoreType.DMA((13,)),
        ],
    )
    near = call(
        near_kernel, [((hid, LANES), BF)] * 2, LIM[9],
        pieces[3], pieces[5], ahead(pieces[FAR], 1), ahead(pieces[8], -1),
    )
    final = [pieces[0], ahead(near[0], 3), ahead(near[1], -3)]
    final += [ahead(pieces[step], step) for step in (2, 6, 1, 7)]
    in_rows = d_in // lax.axis_size(DP)
    grad_in, grad_out, loss = call(
        functools.partial(final_kernel, batch_total=batch_total),
        [((in_rows, hid), F32), ((OUT_COLS, hid), F32), ((1, 1), F32)],
        LIM[8], *final,
    )
    return (loss.reshape(1), grad_in, grad_out.T)


def solution(mesh):
    fine = Mesh(mesh.devices.reshape(2, -1, 2, mesh.devices.shape[1] // 2, 2), DP + MP)
    in_specs = (P(DP, None), P(DP, None), P(None, MP), P(MP, None), P())
    out_specs = (P(), P(DP, MP), P(MP, DP))
    return jax.shard_map(
        on_device, mesh=fine, in_specs=in_specs, out_specs=out_specs, check_vma=False
    )
```

```python
import functools

import jax
import jax.numpy as jnp
from jax import lax
from jax.experimental import pallas as pl
from jax.experimental.pallas import tpu as pltpu
from jax.sharding import Mesh, PartitionSpec as P

EPS = 1e-06
GELU_C = 0.7978845608
GELU_K = 0.044715
MP = ("y", "x_hi")
DP = ("x_lo", "z", "core")
PLANE = ("x_lo", "core", "y", "x_hi")
SPREAD = ("x_lo", "y", "x_hi")
BF = jnp.bfloat16
F32 = jnp.float32
LANES = 128
OUT_COLS = 16
FAR = 4
MIB = 1 << 20
LIM = (60, 60, 60, 8, 8, 60, 60, 60, 16, 16)
NT = (((1,), (1,)), ((), ()))


def gelu_val(values, tanh_val):
    return 0.5 * values * (1.0 + tanh_val)


def gelu_der(values, tanh_val):
    return 0.5 * (1.0 + tanh_val) + 0.5 * values * (1.0 - tanh_val * tanh_val) * GELU_C * (
        1.0 + 3.0 * GELU_K * values * values
    )


def gelu_tanh(values):
    return jnp.tanh(GELU_C * (values + GELU_K * values * values * values))


def swap(value, axis):
    return lax.ppermute(value, axis, [(0, 1), (1, 0)])


def exchange(value, axis):
    return lax.all_to_all(value, axis, 0, 0)


def split3(value):
    first = value.astype(BF).astype(F32)
    second = (value - first).astype(BF).astype(F32)
    return first, second, value - first - second


def call(kernel, outs, vmem, *args, scalars=0, scratch=(), after=(), raw=False, direct=False):
    raw = raw or direct
    held = [] if raw else list(args[scalars:])
    total = len(args) + len(after)

    def body(*refs):
        outputs = refs[total : total + len(outs)]
        rest = refs[total + len(outs) :]
        if raw:
            kernel(*refs[: len(args)], *outputs, *rest)
            return
        places, sems, rest = rest[: len(held)], rest[len(held)], rest[len(held) + 1 :]
        copies = [
            pltpu.make_async_copy(refs[scalars + i], places[i], sems.at[i])
            for i in range(len(held))
        ]
        for copy in copies:
            copy.start()
        for copy in copies:
            copy.wait()
        kernel(*refs[:scalars], *places, *outputs, *rest)

    places = [pltpu.VMEM(a.shape, a.dtype) for a in held]
    if held:
        places.append(pltpu.SemaphoreType.DMA((len(held),)))
    anywhere = pl.BlockSpec(memory_space=pl.ANY)
    place = pl.BlockSpec(memory_space=pltpu.VMEM) if direct else anywhere
    return pl.pallas_call(
        body,
        grid=(1,),
        out_shape=[jax.ShapeDtypeStruct(s, d) for s, d in outs],
        in_specs=[pl.BlockSpec(memory_space=pltpu.SMEM)] * scalars
        + [place] * (len(args) - scalars) + [anywhere] * len(after),
        out_specs=[whole(s) for s, _ in outs],
        scratch_shapes=[*places, *scratch],
        compiler_params=pltpu.CompilerParams(vmem_limit_bytes=vmem * MIB),
        cost_estimate=pl.CostEstimate(flops=1024, bytes_accessed=1024, transcendentals=0),
    )(*args, *after)


def whole(shape):
    return pl.BlockSpec(shape, lambda i: (0,) * len(shape), pipeline_mode=pl.Buffered(1))


def gate(first, *arrays, after=()):
    after = (first, *after)
    anywhere = pl.BlockSpec(memory_space=pl.ANY)
    return pl.pallas_call(
        lambda *refs: None,
        out_shape=[jax.ShapeDtypeStruct(a.shape, a.dtype) for a in arrays],
        in_specs=[anywhere] * (len(arrays) + len(after)),
        out_specs=[anywhere] * len(arrays),
        input_output_aliases={i + len(after): i for i in range(len(arrays))},
        compiler_params=pltpu.CompilerParams(vmem_limit_bytes=60 * MIB),
    )(*after, *arrays)


def parts_of(size, count):
    step = -(-size // (16 * count)) * 16
    return [slice(i, min(i + step, size)) for i in range(0, size, step)]


def head_kernel(
    text_hbm, feats_hbm, win_hbm, wout_hbm, partial_ref, pre_ref, emb_ref,
    text_ref, feats_ref, win_ref, wout_ref, hidden_ref, sems,
):
    spans = parts_of(win_ref.shape[0], 1)
    copies = [
        pltpu.make_async_copy(text_hbm, text_ref, sems.at[0]),
        pltpu.make_async_copy(feats_hbm, feats_ref, sems.at[1]),
    ]
    copies += [
        pltpu.make_async_copy(win_hbm.at[span], win_ref.at[span], sems.at[3 + i])
        for i, span in enumerate(spans)
    ]
    copies.append(pltpu.make_async_copy(wout_hbm, wout_ref, sems.at[2]))
    for copy in copies:
        copy.start()
    copies[0].wait()
    text = text_ref[...].astype(F32)
    emb_ref[...] = (text * lax.rsqrt(jnp.sum(text * text, axis=-1, keepdims=True) + EPS)).astype(BF)
    copies[1].wait()
    for i, span in enumerate(spans):
        copies[2 + i].wait()
        pre = lax.dot_general(win_ref[span, :], feats_ref[...], NT, preferred_element_type=F32)
        hidden_ref[span, :] = gelu_val(pre, gelu_tanh(pre)).astype(BF)
        pre_ref[span, :] = pre.astype(BF)
    copies[-1].wait()
    partial_ref[...] = lax.dot_general(
        hidden_ref[...], wout_ref[...], (((0,), (0,)), ((), ())), preferred_element_type=F32
    ).astype(BF)


def feats_kernel(where_ref, feats_ref, own_ref, give_ref):
    x_index, c_index = where_ref[0], where_ref[1]
    rows, width = feats_ref.shape
    z_count = own_ref.shape[1] // LANES
    chunk = width // (4 * z_count)
    source = lax.broadcasted_iota(jnp.int32, (2 * LANES, LANES), 0)
    target = lax.broadcasted_iota(jnp.int32, (2 * LANES, LANES), 1)
    inside = (target >= OUT_COLS) & (target < OUT_COLS + chunk)
    for rx, rc in [(a, b) for a in range(2) for b in range(2)]:
        for z in range(z_count):
            target_z = lax.rem(where_ref[3] + z, z_count)
            begin = (((rx ^ x_index) * z_count + target_z) * 2 + (rc ^ c_index)) * chunk
            window = jnp.minimum(begin // LANES * LANES, width - 2 * LANES)
            shift = begin - window - OUT_COLS
            move = jnp.where(inside & (source == target + shift), 1.0, 0.0).astype(BF)
            piece = feats_ref[:, pl.ds(pl.multiple_of(window, LANES), 2 * LANES)]
            piece = jnp.dot(piece, move, preferred_element_type=F32).astype(BF)
            out_ref = (own_ref, give_ref)[rx]
            out_ref[rc * rows : (rc + 1) * rows, z * LANES : (z + 1) * LANES] = piece


def unit_kernel(got_ref, unit_ref, inv_ref, spread_ref):
    projected = jnp.sum(got_ref[...].astype(F32), axis=0)
    inv_norm = lax.rsqrt(jnp.sum(projected * projected, axis=-1, keepdims=True) + EPS)
    unit = projected * inv_norm
    unit_ref[...] = unit
    inv_ref[...] = jnp.broadcast_to(inv_norm, inv_ref.shape)
    spread_ref[...] = jnp.broadcast_to(unit.astype(BF)[None], spread_ref.shape)


def expo_block(scale_val, video_ref, text):
    count, own_rows, emb = video_ref.shape
    video = video_ref[...].reshape(count * own_rows, emb)
    return jnp.exp(scale_val * lax.dot_general(video, text, NT, preferred_element_type=F32))


def column_place(where_ref, block):
    return (((block // 2) ^ where_ref[0]) * 2 + ((block % 2) ^ where_ref[1])) * 2


def logits_kernel(where_ref, scale_ref, video_ref, *refs):
    text_refs, (spread_ref, col_ref) = refs[:4], refs[4:]
    for block in range(4):
        expo = expo_block(scale_ref[0], video_ref, text_refs[block][...])
        col_part = jnp.sum(expo, axis=0, keepdims=True)
        for half in range(2):
            col_ref[pl.ds(column_place(where_ref, block) + half, 1), :] = col_part[
                :, half * LANES : (half + 1) * LANES
            ]
    spread_ref[...] = jnp.broadcast_to(col_ref[...][None], spread_ref.shape)


def weights_kernel(where_ref, scale_ref, video_ref, *refs):
    text_refs, (got_ref, packed_ref, log_ref, inv_ref) = refs[:4], refs[4:]
    count, own_rows, emb = video_ref.shape
    rows = count * own_rows
    col_sum = jnp.sum(got_ref[...], axis=0)
    log_ref[...] = jnp.log(col_sum)
    inv_ref[...] = 1.0 / col_sum
    first = jnp.zeros((rows, emb), F32)
    second = jnp.zeros((rows, emb), F32)
    row_part = jnp.zeros((rows, 1), F32)
    for block in range(4):
        text = text_refs[block][...]
        expo = expo_block(scale_ref[0], video_ref, text)
        row_part += jnp.sum(expo, axis=1, keepdims=True)
        place = column_place(where_ref, block)
        inv = jnp.concatenate([inv_ref[pl.ds(place + half, 1), :] for half in range(2)], axis=1)
        first += jnp.dot(expo.astype(BF), text, preferred_element_type=F32)
        second += jnp.dot((expo * inv).astype(BF), text, preferred_element_type=F32)
    packed_ref[:, :, :emb] = first.astype(BF).reshape(count, own_rows, emb)
    packed_ref[:, :, emb : 2 * emb] = second.astype(BF).reshape(count, own_rows, emb)
    row_hi = row_part.astype(BF).astype(F32)
    lane = lax.broadcasted_iota(jnp.int32, (rows, LANES), 1)
    both = jnp.where(lane < LANES // 2, row_hi, row_part - row_hi)
    packed_ref[:, :, 2 * emb :] = both.astype(BF).reshape(count, own_rows, LANES)


def proj_kernel(where_ref, scale_ref, back_ref, unit_ref, inv_ref, text_ref, log_ref, out_ref, *, sharers):
    scale_val = scale_ref[0]
    own_rows, emb = unit_ref.shape
    back = jnp.sum(back_ref[...].astype(F32), axis=0)
    half = 2 * emb + LANES // 2
    row_sum = back[:, 2 * emb : 2 * emb + 1] + back[:, half : half + 1]
    weighted = back[:, :emb] / row_sum + back[:, emb : 2 * emb]
    text = text_ref[where_ref[2]].astype(F32)
    unit = unit_ref[...]
    positive = scale_val * jnp.sum(unit.astype(BF).astype(F32) * text, axis=-1, keepdims=True)
    rows_piece = jnp.sum(jnp.log(row_sum) - 2.0 * positive, axis=0, keepdims=True)
    cols_piece = jnp.sum(jnp.sum(log_ref[...], axis=0, keepdims=True), axis=1, keepdims=True)
    a, b, c = split3(rows_piece + cols_piece / sharers)
    grad_emb = 0.5 * scale_val * weighted - scale_val * text
    grad_proj = inv_ref[:, :1] * (
        grad_emb - unit * jnp.sum(unit * grad_emb, axis=-1, keepdims=True)
    )
    lane = lax.broadcasted_iota(jnp.int32, (own_rows, LANES), 1)
    row = lax.broadcasted_iota(jnp.int32, (own_rows, LANES), 0)
    loss = jnp.where(lane == 0, a, jnp.where(lane == 1, b, jnp.where(lane == 2, c, 0.0)))
    loss = jnp.where(row == 0, loss, 0.0)
    sent = jnp.concatenate([grad_proj, loss], axis=1).astype(BF)
    out_ref[...] = jnp.broadcast_to(sent[None], out_ref.shape)


def gelu_kernel(*refs):
    pre_refs, (hidden_ref, der_ref) = refs[:4], refs[4:]
    rows = pre_refs[0].shape[1]
    for block in range(4):
        pre = pre_refs[block][...].astype(F32)
        tanh_val = gelu_tanh(pre)
        span = slice(block * rows, (block + 1) * rows)
        hidden_ref[:, span] = gelu_val(pre, tanh_val).astype(BF)
        der_ref[:, span] = gelu_der(pre, tanh_val).astype(BF)


def grads_kernel(where_ref, own_hbm, other_hbm, wout_hbm, hidden_hbm, der_hbm, *refs):
    feats_hbm, out_refs, refs = refs[:4], refs[4:13], refs[13:]
    grads_ref, wout_ref, der_ref, hidden_ref, feats_ref, sems = refs
    x_index, c_index = where_ref[0], where_ref[1]
    rows = own_hbm.shape[1]
    hid, emb = wout_ref.shape
    z_count = feats_ref.shape[1] // LANES
    spans = parts_of(hid, 2)
    copies = []
    for block in range(4):
        rx, rc = block // 2, block % 2
        source = other_hbm if rc else own_hbm
        copies.append((source.at[rx ^ x_index], grads_ref.at[block]))
    copies.append((wout_hbm, wout_ref))
    copies.append((der_hbm.at[spans[0]], der_ref.at[spans[0]]))
    for block in range(4):
        side = pl.ds(block % 2 * rows, rows)
        copies.append((feats_hbm[block].at[side], feats_ref.at[pl.ds(block * rows, rows)]))
    copies.append((hidden_hbm.at[spans[0]], hidden_ref.at[spans[0]]))
    copies.append((der_hbm.at[spans[1]], der_ref.at[spans[1]]))
    copies.append((hidden_hbm.at[spans[1]], hidden_ref.at[spans[1]]))
    copies = [pltpu.make_async_copy(a, b, sems.at[i]) for i, (a, b) in enumerate(copies)]
    for copy in copies:
        copy.start()
    source = lax.broadcasted_iota(jnp.int32, (emb, LANES), 0)
    target = lax.broadcasted_iota(jnp.int32, (emb, LANES), 1)
    column = lax.rem(where_ref[3] + target // OUT_COLS, z_count) * 2 + c_index
    column = x_index * (emb // 2) + column * OUT_COLS + target % OUT_COLS
    pick = jnp.where(source == column, 1.0, 0.0).astype(BF)
    for copy in copies[:5]:
        copy.wait()
    grads = grads_ref[:, :, :emb].reshape(4 * rows, emb)
    picked = jnp.dot(grads, pick, preferred_element_type=F32).astype(BF)
    loss = jnp.zeros((1, LANES), F32)
    for block in range(4):
        loss += jnp.sum(grads_ref[block, :, emb:].astype(F32), axis=0, keepdims=True)
    a, b, c = split3(jnp.sum(loss, axis=1, keepdims=True))
    for i, span in enumerate(spans):
        size = span.stop - span.start
        lane = lax.broadcasted_iota(jnp.int32, (size, LANES), 1)
        grad_hidden = lax.dot_general(wout_ref[span, :], grads, NT, preferred_element_type=F32)
        copies[(5, 11)[i]].wait()
        grad_pre = (grad_hidden * der_ref[span, :].astype(F32)).astype(BF)
        if i == 0:
            for copy in copies[6:10]:
                copy.wait()
        total = jnp.dot(grad_pre, feats_ref[...], preferred_element_type=F32)
        copies[(10, 12)[i]].wait()
        outer = jnp.dot(hidden_ref[span, :], picked, preferred_element_type=F32)
        for z in range(z_count):
            moved = outer if z == 0 else pltpu.roll(outer, LANES - z * OUT_COLS, 1)
            value = jnp.where(lane < OUT_COLS, moved, total[:, z * LANES : (z + 1) * LANES])
            if i == 0:
                row = lax.broadcasted_iota(jnp.int32, (size, LANES), 0)
                extra = jnp.where(row == 0, a, jnp.where(row == 1, b, c))
                value = jnp.where((lane == LANES - 1) & (row < 3), extra, value)
            if z == FAR:
                out_refs[FAR + 4 * i][...] = value.astype(BF)
            else:
                out_refs[z][span, :] = value.astype(BF)


def near_kernel(up_ref, down_ref, up_far_ref, down_far_ref, up_out, down_out):
    first = up_far_ref.shape[0]
    up_out[:first] = (up_ref[:first].astype(F32) + up_far_ref[...].astype(F32)).astype(BF)
    up_out[first:] = up_ref[first:]
    down_out[:first] = down_ref[:first]
    down_out[first:] = (down_ref[first:].astype(F32) + down_far_ref[...].astype(F32)).astype(BF)


def final_kernel(*refs, batch_total):
    got, (in_ref, out_ref, loss_ref) = refs[:7], refs[7:]
    total = got[0][...].astype(F32)
    for ref in got[1:]:
        total += ref[...].astype(F32)
    turned = total.T
    in_rows = in_ref.shape[0]
    out_ref[...] = turned[:OUT_COLS]
    in_ref[...] = turned[OUT_COLS : OUT_COLS + in_rows]
    loss = jnp.sum(total[:3, LANES - 1 :], axis=0, keepdims=True) / (2.0 * batch_total)
    loss_ref[...] = loss


def ahead(value, step):
    return lax.ppermute(value, "z", [(i, (i + step) % 8) for i in range(8)])


def on_device(video_feats, text_feats, weight_in, weight_out, logit_scale):
    rows, d_in = video_feats.shape
    hid, emb = weight_out.shape
    mp_count = lax.axis_size(MP)
    own_rows = rows // mp_count
    batch_total = rows * lax.axis_size(DP)
    where = [lax.axis_index(name) for name in ("x_lo", "core", MP, "z")]
    where = jnp.stack(where).astype(jnp.int32)

    partial_value, pre_bf, text_emb = call(
        head_kernel, [((rows, emb), BF), ((hid, rows), BF), ((rows, emb), BF)], LIM[0],
        text_feats, video_feats, weight_in.T, weight_out, raw=True,
        scratch=[
            pltpu.VMEM((rows, emb), BF), pltpu.VMEM((rows, d_in), BF), pltpu.VMEM((hid, d_in), BF),
            pltpu.VMEM((hid, emb), BF), pltpu.VMEM((hid, rows), BF), pltpu.SemaphoreType.DMA((6,)),
        ],
    )
    got = exchange(partial_value.reshape(mp_count, own_rows, emb), MP)

    text_x = swap(text_emb, "x_lo")
    texts = [swap(text_emb, "core"), text_x, swap(text_x, "core")]
    z_count = lax.axis_size("z")
    feats, give_x = call(
        feats_kernel, [((2 * rows, z_count * LANES), BF)] * 2, LIM[1], where, video_feats, scalars=1
    )
    unit, inv_norm, video = call(
        unit_kernel,
        [((own_rows, emb), F32), ((own_rows, LANES), F32), ((8, own_rows, emb), BF)],
        LIM[2], got, after=(feats, text_x),
    )
    give_x, pre_own = gate(inv_norm, give_x, pre_bf)
    feats_x = swap(give_x, "x_lo")

    video_rows = exchange(video, "z")
    (cols,) = call(
        logits_kernel, [((4 * mp_count, 8, LANES), F32)], LIM[3],
        where, logit_scale, video_rows, text_emb, *texts, scalars=2, direct=True,
        scratch=[pltpu.VMEM((8, LANES), F32)],
    )
    cols = exchange(cols, PLANE)
    pre_x = swap(pre_own, "x_lo")
    pre = (pre_own, swap(pre_own, "core"), pre_x, swap(pre_x, "core"))
    packed, logs = call(
        weights_kernel, [((8, own_rows, 2 * emb + LANES), BF), ((8, LANES), F32)], LIM[4],
        where, logit_scale, video_rows, text_emb, *texts, cols, scalars=2, direct=True,
        scratch=[pltpu.VMEM((8, LANES), F32)],
    )
    feats_q = (feats, swap(feats, "core"), feats_x, swap(feats_x, "core"))
    back = exchange(packed, "z")
    (sent,) = call(
        functools.partial(proj_kernel, sharers=4 * mp_count),
        [((2 * mp_count, own_rows, emb + LANES), BF)], LIM[5],
        where, logit_scale, back, unit, inv_norm, text_emb.reshape(mp_count, own_rows, emb), logs,
        scalars=2, after=(feats_q[1], feats_q[3], pre[1], pre[3]),
    )
    gelus = call(gelu_kernel, [((hid, 4 * rows), BF)] * 2, LIM[6], *pre, after=(sent,))
    grads = exchange(sent, SPREAD).reshape(2, rows, emb + LANES)
    (grads,) = gate(gelus[0], grads, after=(gelus[1],))
    other = swap(grads, "core")
    first = parts_of(hid, 2)[0].stop
    sizes = [hid] * FAR + [first] + [hid] * (7 - FAR) + [hid - first]
    pieces = call(
        grads_kernel, [((size, LANES), BF) for size in sizes], LIM[7],
        where, grads, other, weight_out, *gelus, *feats_q, scalars=1, raw=True,
        scratch=[
            pltpu.VMEM((4, rows, emb + LANES), BF), pltpu.VMEM((hid, emb), BF),
            pltpu.VMEM((hid, 4 * rows), BF), pltpu.VMEM((hid, 4 * rows), BF),
            pltpu.VMEM((4 * rows, z_count * LANES), BF), pltpu.SemaphoreType.DMA((13,)),
        ],
    )
    near = call(
        near_kernel, [((hid, LANES), BF)] * 2, LIM[9],
        pieces[3], pieces[5], ahead(pieces[FAR], 1), ahead(pieces[8], -1), direct=True,
    )
    final = [pieces[0], ahead(near[0], 3), ahead(near[1], -3)]
    final += [ahead(pieces[step], step) for step in (2, 6, 1, 7)]
    in_rows = d_in // lax.axis_size(DP)
    grad_in, grad_out, loss = call(
        functools.partial(final_kernel, batch_total=batch_total),
        [((in_rows, hid), F32), ((OUT_COLS, hid), F32), ((1, 1), F32)],
        LIM[8], *final, direct=True,
    )
    return (loss.reshape(1), grad_in, grad_out.T)


def solution(mesh):
    fine = Mesh(mesh.devices.reshape(2, -1, 2, mesh.devices.shape[1] // 2, 2), DP + MP)
    in_specs = (P(DP, None), P(DP, None), P(None, MP), P(MP, None), P())
    out_specs = (P(), P(DP, MP), P(MP, DP))
    return jax.shard_map(
        on_device, mesh=fine, in_specs=in_specs, out_specs=out_specs, check_vma=False
    )
```

```python
import functools

import jax
import jax.numpy as jnp
from jax import lax
from jax.experimental import pallas as pl
from jax.experimental.pallas import tpu as pltpu
from jax.sharding import Mesh, PartitionSpec as P

EPS = 1e-06
GELU_C = 0.7978845608
GELU_K = 0.044715
MP = ("y", "x_hi")
DP = ("x_lo", "z", "core")
PLANE = ("x_lo", "core", "y", "x_hi")
SPREAD = ("x_lo", "y", "x_hi")
BF = jnp.bfloat16
F32 = jnp.float32
LANES = 128
OUT_COLS = 16
FAR = 4
EXTRA = 16
MIB = 1 << 20
LIM = (60, 60, 60, 8, 8, 60, 60, 60, 16, 16)
NT = (((1,), (1,)), ((), ()))


def gelu_val(values, tanh_val):
    return 0.5 * values * (1.0 + tanh_val)


def gelu_der(values, tanh_val):
    return 0.5 * (1.0 + tanh_val) + 0.5 * values * (1.0 - tanh_val * tanh_val) * GELU_C * (
        1.0 + 3.0 * GELU_K * values * values
    )


def gelu_tanh(values):
    return jnp.tanh(GELU_C * (values + GELU_K * values * values * values))


def swap(value, axis):
    return lax.ppermute(value, axis, [(0, 1), (1, 0)])


def exchange(value, axis):
    return lax.all_to_all(value, axis, 0, 0)


def split3(value):
    first = value.astype(BF).astype(F32)
    second = (value - first).astype(BF).astype(F32)
    return first, second, value - first - second


def call(kernel, outs, vmem, *args, scalars=0, scratch=(), after=(), raw=False, direct=False):
    raw = raw or direct
    held = [] if raw else list(args[scalars:])
    total = len(args) + len(after)

    def body(*refs):
        outputs = refs[total : total + len(outs)]
        rest = refs[total + len(outs) :]
        if raw:
            kernel(*refs[: len(args)], *outputs, *rest)
            return
        places, sems, rest = rest[: len(held)], rest[len(held)], rest[len(held) + 1 :]
        copies = [
            pltpu.make_async_copy(refs[scalars + i], places[i], sems.at[i])
            for i in range(len(held))
        ]
        for copy in copies:
            copy.start()
        for copy in copies:
            copy.wait()
        kernel(*refs[:scalars], *places, *outputs, *rest)

    places = [pltpu.VMEM(a.shape, a.dtype) for a in held]
    if held:
        places.append(pltpu.SemaphoreType.DMA((len(held),)))
    anywhere = pl.BlockSpec(memory_space=pl.ANY)
    place = pl.BlockSpec(memory_space=pltpu.VMEM) if direct else anywhere
    return pl.pallas_call(
        body,
        grid=(1,),
        out_shape=[jax.ShapeDtypeStruct(s, d) for s, d in outs],
        in_specs=[pl.BlockSpec(memory_space=pltpu.SMEM)] * scalars
        + [place] * (len(args) - scalars) + [anywhere] * len(after),
        out_specs=[whole(s) for s, _ in outs],
        scratch_shapes=[*places, *scratch],
        compiler_params=pltpu.CompilerParams(vmem_limit_bytes=vmem * MIB),
        cost_estimate=pl.CostEstimate(flops=1024, bytes_accessed=1024, transcendentals=0),
    )(*args, *after)


def whole(shape):
    return pl.BlockSpec(shape, lambda i: (0,) * len(shape), pipeline_mode=pl.Buffered(1))


def gate(first, *arrays, after=()):
    after = (first, *after)
    anywhere = pl.BlockSpec(memory_space=pl.ANY)
    return pl.pallas_call(
        lambda *refs: None,
        out_shape=[jax.ShapeDtypeStruct(a.shape, a.dtype) for a in arrays],
        in_specs=[anywhere] * (len(arrays) + len(after)),
        out_specs=[anywhere] * len(arrays),
        input_output_aliases={i + len(after): i for i in range(len(arrays))},
        compiler_params=pltpu.CompilerParams(vmem_limit_bytes=60 * MIB),
    )(*after, *arrays)


def parts_of(size, count):
    step = -(-size // (16 * count)) * 16
    return [slice(i, min(i + step, size)) for i in range(0, size, step)]


def head_kernel(
    text_hbm, feats_hbm, win_hbm, wout_hbm, partial_ref, pre_ref, emb_ref,
    text_ref, feats_ref, win_ref, wout_ref, hidden_ref, sems,
):
    spans = parts_of(win_ref.shape[0], 1)
    copies = [
        pltpu.make_async_copy(text_hbm, text_ref, sems.at[0]),
        pltpu.make_async_copy(feats_hbm, feats_ref, sems.at[1]),
    ]
    copies += [
        pltpu.make_async_copy(win_hbm.at[span], win_ref.at[span], sems.at[3 + i])
        for i, span in enumerate(spans)
    ]
    copies.append(pltpu.make_async_copy(wout_hbm, wout_ref, sems.at[2]))
    for copy in copies:
        copy.start()
    copies[0].wait()
    text = text_ref[...].astype(F32)
    emb_ref[...] = (text * lax.rsqrt(jnp.sum(text * text, axis=-1, keepdims=True) + EPS)).astype(BF)
    copies[1].wait()
    for i, span in enumerate(spans):
        copies[2 + i].wait()
        pre = lax.dot_general(win_ref[span, :], feats_ref[...], NT, preferred_element_type=F32)
        hidden_ref[span, :] = gelu_val(pre, gelu_tanh(pre)).astype(BF)
        pre_ref[span, :] = pre.astype(BF)
    copies[-1].wait()
    partial_ref[...] = lax.dot_general(
        hidden_ref[...], wout_ref[...], (((0,), (0,)), ((), ())), preferred_element_type=F32
    ).astype(BF)


def feats_kernel(where_ref, feats_ref, own_ref, give_ref):
    x_index, c_index = where_ref[0], where_ref[1]
    rows, width = feats_ref.shape
    z_count = own_ref.shape[1] // LANES
    chunk = width // (4 * z_count)
    source = lax.broadcasted_iota(jnp.int32, (2 * LANES, LANES), 0)
    target = lax.broadcasted_iota(jnp.int32, (2 * LANES, LANES), 1)
    inside = (target >= OUT_COLS) & (target < OUT_COLS + chunk)
    for rx, rc in [(a, b) for a in range(2) for b in range(2)]:
        for z in range(z_count):
            target_z = lax.rem(where_ref[3] + z, z_count)
            begin = (((rx ^ x_index) * z_count + target_z) * 2 + (rc ^ c_index)) * chunk
            window = jnp.minimum(begin // LANES * LANES, width - 2 * LANES)
            shift = begin - window - OUT_COLS
            move = jnp.where(inside & (source == target + shift), 1.0, 0.0).astype(BF)
            piece = feats_ref[:, pl.ds(pl.multiple_of(window, LANES), 2 * LANES)]
            piece = jnp.dot(piece, move, preferred_element_type=F32).astype(BF)
            out_ref = (own_ref, give_ref)[rx]
            out_ref[rc * rows : (rc + 1) * rows, z * LANES : (z + 1) * LANES] = piece


def unit_kernel(got_ref, unit_ref, inv_ref, spread_ref):
    projected = jnp.sum(got_ref[...].astype(F32), axis=0)
    inv_norm = lax.rsqrt(jnp.sum(projected * projected, axis=-1, keepdims=True) + EPS)
    unit = projected * inv_norm
    unit_ref[...] = unit
    inv_ref[...] = jnp.broadcast_to(inv_norm, inv_ref.shape)
    spread_ref[...] = jnp.broadcast_to(unit.astype(BF)[None], spread_ref.shape)


def expo_block(scale_val, video_ref, text):
    count, own_rows, emb = video_ref.shape
    video = video_ref[...].reshape(count * own_rows, emb)
    return jnp.exp(scale_val * lax.dot_general(video, text, NT, preferred_element_type=F32))


def column_place(where_ref, block):
    return (((block // 2) ^ where_ref[0]) * 2 + ((block % 2) ^ where_ref[1])) * 2


def logits_kernel(where_ref, scale_ref, video_ref, *refs):
    text_refs, (spread_ref, col_ref) = refs[:4], refs[4:]
    for block in range(4):
        expo = expo_block(scale_ref[0], video_ref, text_refs[block][...])
        col_part = jnp.sum(expo, axis=0, keepdims=True)
        for half in range(2):
            col_ref[pl.ds(column_place(where_ref, block) + half, 1), :] = col_part[
                :, half * LANES : (half + 1) * LANES
            ]
    spread_ref[...] = jnp.broadcast_to(col_ref[...][None], spread_ref.shape)


def weights_kernel(where_ref, scale_ref, video_ref, *refs):
    text_refs, (got_ref, packed_ref, log_ref, inv_ref) = refs[:4], refs[4:]
    count, own_rows, emb = video_ref.shape
    rows = count * own_rows
    col_sum = jnp.sum(got_ref[...], axis=0)
    log_ref[...] = jnp.log(col_sum)
    inv_ref[...] = 1.0 / col_sum
    first = jnp.zeros((rows, emb), F32)
    second = jnp.zeros((rows, emb), F32)
    row_part = jnp.zeros((rows, 1), F32)
    for block in range(4):
        text = text_refs[block][...]
        expo = expo_block(scale_ref[0], video_ref, text)
        row_part += jnp.sum(expo, axis=1, keepdims=True)
        place = column_place(where_ref, block)
        inv = jnp.concatenate([inv_ref[pl.ds(place + half, 1), :] for half in range(2)], axis=1)
        first += jnp.dot(expo.astype(BF), text, preferred_element_type=F32)
        second += jnp.dot((expo * inv).astype(BF), text, preferred_element_type=F32)
    tiles = emb // LANES
    for i, side in enumerate((first, second)):
        for tile in range(tiles):
            begin = (i * tiles + tile) * own_rows
            part = side[:, tile * LANES : (tile + 1) * LANES]
            packed_ref[:, begin : begin + own_rows, :] = part.astype(BF).reshape(count, own_rows, LANES)
    row_hi = row_part.astype(BF).astype(F32)
    row_lo = (row_part - row_hi).reshape(count, own_rows, 1)
    row_hi = row_hi.reshape(count, own_rows, 1)
    row = lax.broadcasted_iota(jnp.int32, (count, own_rows, LANES), 1)
    lane = lax.broadcasted_iota(jnp.int32, (count, own_rows, LANES), 2)
    turned = jnp.where(lane == row, row_hi, jnp.where(lane == row + own_rows, row_lo, 0.0))
    turned = jnp.sum(turned, axis=1, keepdims=True)
    packed_ref[:, 2 * tiles * own_rows :, :] = jnp.broadcast_to(turned, (count, EXTRA, LANES)).astype(BF)


def proj_kernel(where_ref, scale_ref, back_ref, unit_ref, inv_ref, text_ref, log_ref, out_ref, *, sharers):
    scale_val = scale_ref[0]
    own_rows, emb = unit_ref.shape
    back = jnp.sum(back_ref[...].astype(F32), axis=0)
    tiles = emb // LANES
    parts = [back[i * own_rows : (i + 1) * own_rows] for i in range(2 * tiles)]
    lane = lax.broadcasted_iota(jnp.int32, (own_rows, LANES), 1)
    row = lax.broadcasted_iota(jnp.int32, (own_rows, LANES), 0)
    sums = back[2 * tiles * own_rows : 2 * tiles * own_rows + 1]
    sums = jnp.where((lane == row) | (lane == row + own_rows), sums, 0.0)
    row_sum = jnp.sum(sums, axis=1, keepdims=True)
    weighted = jnp.concatenate(parts[:tiles], axis=1) / row_sum + jnp.concatenate(parts[tiles:], axis=1)
    text = text_ref[where_ref[2]].astype(F32)
    unit = unit_ref[...]
    positive = scale_val * jnp.sum(unit.astype(BF).astype(F32) * text, axis=-1, keepdims=True)
    rows_piece = jnp.sum(jnp.log(row_sum) - 2.0 * positive, axis=0, keepdims=True)
    cols_piece = jnp.sum(jnp.sum(log_ref[...], axis=0, keepdims=True), axis=1, keepdims=True)
    a, b, c = split3(rows_piece + cols_piece / sharers)
    grad_emb = 0.5 * scale_val * weighted - scale_val * text
    grad_proj = inv_ref[:, :1] * (
        grad_emb - unit * jnp.sum(unit * grad_emb, axis=-1, keepdims=True)
    )
    lane, row = lane[:EXTRA], row[:EXTRA]
    loss = jnp.where(lane == 0, a, jnp.where(lane == 1, b, jnp.where(lane == 2, c, 0.0)))
    loss = jnp.where(row == 0, loss, 0.0)
    sent = [grad_proj[:, i * LANES : (i + 1) * LANES] for i in range(tiles)]
    sent = jnp.concatenate(sent + [loss], axis=0).astype(BF)
    out_ref[...] = jnp.broadcast_to(sent[None], out_ref.shape)


def gelu_kernel(*refs):
    pre_refs, (hidden_ref, der_ref) = refs[:4], refs[4:]
    rows = pre_refs[0].shape[1]
    for block in range(4):
        pre = pre_refs[block][...].astype(F32)
        tanh_val = gelu_tanh(pre)
        span = slice(block * rows, (block + 1) * rows)
        hidden_ref[:, span] = gelu_val(pre, tanh_val).astype(BF)
        der_ref[:, span] = gelu_der(pre, tanh_val).astype(BF)


def grads_kernel(where_ref, own_hbm, other_hbm, wout_hbm, hidden_hbm, der_hbm, *refs):
    feats_hbm, out_refs, refs = refs[:4], refs[4:13], refs[13:]
    grads_ref, loss_ref, wout_ref, der_ref, hidden_ref, feats_ref, sems = refs
    x_index, c_index = where_ref[0], where_ref[1]
    _, mp_count, own_rows, _ = grads_ref.shape
    rows = mp_count * own_rows
    hid, emb = wout_ref.shape
    tiles = emb // LANES
    z_count = feats_ref.shape[1] // LANES
    spans = parts_of(hid, 2)
    copies = []
    for block in range(4):
        rx, rc = block // 2, block % 2
        source = other_hbm if rc else own_hbm
        source = source.at[rx ^ x_index]
        for tile in range(tiles):
            place = grads_ref.at[block, :, :, pl.ds(tile * LANES, LANES)]
            copies.append((source.at[:, pl.ds(tile * own_rows, own_rows), :], place))
        copies.append((source.at[:, pl.ds(tiles * own_rows, EXTRA), :], loss_ref.at[block]))
    ready = len(copies) + 1
    copies.append((wout_hbm, wout_ref))
    copies.append((der_hbm.at[spans[0]], der_ref.at[spans[0]]))
    for block in range(4):
        side = pl.ds(block % 2 * rows, rows)
        copies.append((feats_hbm[block].at[side], feats_ref.at[pl.ds(block * rows, rows)]))
    copies.append((hidden_hbm.at[spans[0]], hidden_ref.at[spans[0]]))
    copies.append((der_hbm.at[spans[1]], der_ref.at[spans[1]]))
    copies.append((hidden_hbm.at[spans[1]], hidden_ref.at[spans[1]]))
    copies = [pltpu.make_async_copy(a, b, sems.at[i]) for i, (a, b) in enumerate(copies)]
    for copy in copies:
        copy.start()
    source = lax.broadcasted_iota(jnp.int32, (emb, LANES), 0)
    target = lax.broadcasted_iota(jnp.int32, (emb, LANES), 1)
    column = lax.rem(where_ref[3] + target // OUT_COLS, z_count) * 2 + c_index
    column = x_index * (emb // 2) + column * OUT_COLS + target % OUT_COLS
    pick = jnp.where(source == column, 1.0, 0.0).astype(BF)
    for copy in copies[:ready]:
        copy.wait()
    grads = grads_ref[...].reshape(4 * rows, emb)
    picked = jnp.dot(grads, pick, preferred_element_type=F32).astype(BF)
    loss = jnp.zeros((1, LANES), F32)
    for block in range(4):
        part = loss_ref[block].reshape(mp_count * EXTRA, LANES).astype(F32)
        loss += jnp.sum(part, axis=0, keepdims=True)
    a, b, c = split3(jnp.sum(loss, axis=1, keepdims=True))
    for i, span in enumerate(spans):
        size = span.stop - span.start
        lane = lax.broadcasted_iota(jnp.int32, (size, LANES), 1)
        grad_hidden = lax.dot_general(wout_ref[span, :], grads, NT, preferred_element_type=F32)
        copies[ready + (0, 6)[i]].wait()
        grad_pre = (grad_hidden * der_ref[span, :].astype(F32)).astype(BF)
        if i == 0:
            for copy in copies[ready + 1 : ready + 5]:
                copy.wait()
        total = jnp.dot(grad_pre, feats_ref[...], preferred_element_type=F32)
        copies[ready + (5, 7)[i]].wait()
        outer = jnp.dot(hidden_ref[span, :], picked, preferred_element_type=F32)
        for z in range(z_count):
            moved = outer if z == 0 else pltpu.roll(outer, LANES - z * OUT_COLS, 1)
            value = jnp.where(lane < OUT_COLS, moved, total[:, z * LANES : (z + 1) * LANES])
            if i == 0:
                row = lax.broadcasted_iota(jnp.int32, (size, LANES), 0)
                extra = jnp.where(row == 0, a, jnp.where(row == 1, b, c))
                value = jnp.where((lane == LANES - 1) & (row < 3), extra, value)
            if z == FAR:
                out_refs[FAR + 4 * i][...] = value.astype(BF)
            else:
                out_refs[z][span, :] = value.astype(BF)


def near_kernel(up_ref, down_ref, up_far_ref, down_far_ref, up_out, down_out):
    first = up_far_ref.shape[0]
    up_out[:first] = (up_ref[:first].astype(F32) + up_far_ref[...].astype(F32)).astype(BF)
    up_out[first:] = up_ref[first:]
    down_out[:first] = down_ref[:first]
    down_out[first:] = (down_ref[first:].astype(F32) + down_far_ref[...].astype(F32)).astype(BF)


def final_kernel(*refs, batch_total):
    got, (in_ref, out_ref, loss_ref) = refs[:7], refs[7:]
    total = got[0][...].astype(F32)
    for ref in got[1:]:
        total += ref[...].astype(F32)
    turned = total.T
    in_rows = in_ref.shape[0]
    out_ref[...] = turned[:OUT_COLS]
    in_ref[...] = turned[OUT_COLS : OUT_COLS + in_rows]
    loss = jnp.sum(total[:3, LANES - 1 :], axis=0, keepdims=True) / (2.0 * batch_total)
    loss_ref[...] = loss


def ahead(value, step):
    return lax.ppermute(value, "z", [(i, (i + step) % 8) for i in range(8)])


def on_device(video_feats, text_feats, weight_in, weight_out, logit_scale):
    rows, d_in = video_feats.shape
    hid, emb = weight_out.shape
    mp_count = lax.axis_size(MP)
    own_rows = rows // mp_count
    packs = own_rows * (emb // LANES)
    batch_total = rows * lax.axis_size(DP)
    where = [lax.axis_index(name) for name in ("x_lo", "core", MP, "z")]
    where = jnp.stack(where).astype(jnp.int32)

    partial_value, pre_bf, text_emb = call(
        head_kernel, [((rows, emb), BF), ((hid, rows), BF), ((rows, emb), BF)], LIM[0],
        text_feats, video_feats, weight_in.T, weight_out, raw=True,
        scratch=[
            pltpu.VMEM((rows, emb), BF), pltpu.VMEM((rows, d_in), BF), pltpu.VMEM((hid, d_in), BF),
            pltpu.VMEM((hid, emb), BF), pltpu.VMEM((hid, rows), BF), pltpu.SemaphoreType.DMA((6,)),
        ],
    )
    got = exchange(partial_value.reshape(mp_count, own_rows, emb), MP)

    text_x = swap(text_emb, "x_lo")
    texts = [swap(text_emb, "core"), text_x, swap(text_x, "core")]
    z_count = lax.axis_size("z")
    feats, give_x = call(
        feats_kernel, [((2 * rows, z_count * LANES), BF)] * 2, LIM[1], where, video_feats, scalars=1
    )
    unit, inv_norm, video = call(
        unit_kernel,
        [((own_rows, emb), F32), ((own_rows, LANES), F32), ((8, own_rows, emb), BF)],
        LIM[2], got, after=(feats, text_x),
    )
    give_x, pre_own = gate(inv_norm, give_x, pre_bf)
    feats_x = swap(give_x, "x_lo")

    video_rows = exchange(video, "z")
    (cols,) = call(
        logits_kernel, [((4 * mp_count, 8, LANES), F32)], LIM[3],
        where, logit_scale, video_rows, text_emb, *texts, scalars=2, direct=True,
        scratch=[pltpu.VMEM((8, LANES), F32)],
    )
    cols = exchange(cols, PLANE)
    pre_x = swap(pre_own, "x_lo")
    pre = (pre_own, swap(pre_own, "core"), pre_x, swap(pre_x, "core"))
    packed, logs = call(
        weights_kernel, [((z_count, 2 * packs + EXTRA, LANES), BF), ((8, LANES), F32)], LIM[4],
        where, logit_scale, video_rows, text_emb, *texts, cols, scalars=2, direct=True,
        scratch=[pltpu.VMEM((8, LANES), F32)],
    )
    feats_q = (feats, swap(feats, "core"), feats_x, swap(feats_x, "core"))
    back = exchange(packed, "z")
    (sent,) = call(
        functools.partial(proj_kernel, sharers=4 * mp_count),
        [((2 * mp_count, packs + EXTRA, LANES), BF)], LIM[5],
        where, logit_scale, back, unit, inv_norm, text_emb.reshape(mp_count, own_rows, emb), logs,
        scalars=2, after=(feats_q[1], feats_q[3], pre[1], pre[3]),
    )
    gelus = call(gelu_kernel, [((hid, 4 * rows), BF)] * 2, LIM[6], *pre, after=(sent,))
    grads = exchange(sent, SPREAD).reshape(2, mp_count, packs + EXTRA, LANES)
    (grads,) = gate(gelus[0], grads, after=(gelus[1],))
    other = swap(grads, "core")
    first = parts_of(hid, 2)[0].stop
    sizes = [hid] * FAR + [first] + [hid] * (7 - FAR) + [hid - first]
    pieces = call(
        grads_kernel, [((size, LANES), BF) for size in sizes], LIM[7],
        where, grads, other, weight_out, *gelus, *feats_q, scalars=1, raw=True,
        scratch=[
            pltpu.VMEM((4, mp_count, own_rows, emb), BF), pltpu.VMEM((4, mp_count, EXTRA, LANES), BF),
            pltpu.VMEM((hid, emb), BF),
            pltpu.VMEM((hid, 4 * rows), BF), pltpu.VMEM((hid, 4 * rows), BF),
            pltpu.VMEM((4 * rows, z_count * LANES), BF), pltpu.SemaphoreType.DMA((29,)),
        ],
    )
    near = call(
        near_kernel, [((hid, LANES), BF)] * 2, LIM[9],
        pieces[3], pieces[5], ahead(pieces[FAR], 1), ahead(pieces[8], -1), direct=True,
    )
    final = [pieces[0], ahead(near[0], 3), ahead(near[1], -3)]
    final += [ahead(pieces[step], step) for step in (2, 6, 1, 7)]
    in_rows = d_in // lax.axis_size(DP)
    grad_in, grad_out, loss = call(
        functools.partial(final_kernel, batch_total=batch_total),
        [((in_rows, hid), F32), ((OUT_COLS, hid), F32), ((1, 1), F32)],
        LIM[8], *final, direct=True,
    )
    return (loss.reshape(1), grad_in, grad_out.T)


def solution(mesh):
    fine = Mesh(mesh.devices.reshape(2, -1, 2, mesh.devices.shape[1] // 2, 2), DP + MP)
    in_specs = (P(DP, None), P(DP, None), P(None, MP), P(MP, None), P())
    out_specs = (P(), P(DP, MP), P(MP, DP))
    return jax.shard_map(
        on_device, mesh=fine, in_specs=in_specs, out_specs=out_specs, check_vma=False
    )
```

```python
import functools

import jax
import jax.numpy as jnp
from jax import lax
from jax.experimental import pallas as pl
from jax.experimental.pallas import tpu as pltpu
from jax.sharding import Mesh, PartitionSpec as P

EPS = 1e-06
GELU_C = 0.7978845608
GELU_K = 0.044715
MP = ("y", "x_hi")
DP = ("x_lo", "z", "core")
PLANE = ("x_lo", "core", "y", "x_hi")
SPREAD = ("x_lo", "y", "x_hi")
BF = jnp.bfloat16
F32 = jnp.float32
LANES = 128
OUT_COLS = 16
FAR = 4
EXTRA = 16
MIB = 1 << 20
LIM = (60, 60, 60, 8, 8, 60, 60, 60, 16, 16)
NT = (((1,), (1,)), ((), ()))


def gelu_val(values, tanh_val):
    return 0.5 * values * (1.0 + tanh_val)


def gelu_der(values, tanh_val):
    return 0.5 * (1.0 + tanh_val) + 0.5 * values * (1.0 - tanh_val * tanh_val) * GELU_C * (
        1.0 + 3.0 * GELU_K * values * values
    )


def gelu_tanh(values):
    return jnp.tanh(GELU_C * (values + GELU_K * values * values * values))


def swap(value, axis):
    return lax.ppermute(value, axis, [(0, 1), (1, 0)])


def exchange(value, axis):
    return lax.all_to_all(value, axis, 0, 0)


def split3(value):
    first = value.astype(BF).astype(F32)
    second = (value - first).astype(BF).astype(F32)
    return first, second, value - first - second


def call(kernel, outs, vmem, *args, scalars=0, scratch=(), after=(), raw=False, direct=False):
    raw = raw or direct
    held = [] if raw else list(args[scalars:])
    total = len(args) + len(after)

    def body(*refs):
        outputs = refs[total : total + len(outs)]
        rest = refs[total + len(outs) :]
        if raw:
            kernel(*refs[: len(args)], *outputs, *rest)
            return
        places, sems, rest = rest[: len(held)], rest[len(held)], rest[len(held) + 1 :]
        copies = [
            pltpu.make_async_copy(refs[scalars + i], places[i], sems.at[i])
            for i in range(len(held))
        ]
        for copy in copies:
            copy.start()
        for copy in copies:
            copy.wait()
        kernel(*refs[:scalars], *places, *outputs, *rest)

    places = [pltpu.VMEM(a.shape, a.dtype) for a in held]
    if held:
        places.append(pltpu.SemaphoreType.DMA((len(held),)))
    anywhere = pl.BlockSpec(memory_space=pl.ANY)
    place = pl.BlockSpec(memory_space=pltpu.VMEM) if direct else anywhere
    return pl.pallas_call(
        body,
        grid=(1,),
        out_shape=[jax.ShapeDtypeStruct(s, d) for s, d in outs],
        in_specs=[pl.BlockSpec(memory_space=pltpu.SMEM)] * scalars
        + [place] * (len(args) - scalars) + [anywhere] * len(after),
        out_specs=[whole(s) for s, _ in outs],
        scratch_shapes=[*places, *scratch],
        compiler_params=pltpu.CompilerParams(vmem_limit_bytes=vmem * MIB),
        cost_estimate=pl.CostEstimate(flops=1024, bytes_accessed=1024, transcendentals=0),
    )(*args, *after)


def whole(shape):
    return pl.BlockSpec(shape, lambda i: (0,) * len(shape), pipeline_mode=pl.Buffered(1))


def gate(first, *arrays, after=()):
    after = (first, *after)
    anywhere = pl.BlockSpec(memory_space=pl.ANY)
    return pl.pallas_call(
        lambda *refs: None,
        out_shape=[jax.ShapeDtypeStruct(a.shape, a.dtype) for a in arrays],
        in_specs=[anywhere] * (len(arrays) + len(after)),
        out_specs=[anywhere] * len(arrays),
        input_output_aliases={i + len(after): i for i in range(len(arrays))},
        compiler_params=pltpu.CompilerParams(vmem_limit_bytes=60 * MIB),
    )(*after, *arrays)


def parts_of(size, count):
    step = -(-size // (16 * count)) * 16
    return [slice(i, min(i + step, size)) for i in range(0, size, step)]


def head_kernel(
    text_hbm, feats_hbm, win_hbm, wout_hbm, partial_ref, pre_ref, emb_ref,
    text_ref, feats_ref, win_ref, wout_ref, hidden_ref, sems,
):
    spans = parts_of(win_ref.shape[0], 1)
    copies = [
        pltpu.make_async_copy(text_hbm, text_ref, sems.at[0]),
        pltpu.make_async_copy(feats_hbm, feats_ref, sems.at[1]),
    ]
    copies += [
        pltpu.make_async_copy(win_hbm.at[span], win_ref.at[span], sems.at[3 + i])
        for i, span in enumerate(spans)
    ]
    copies.append(pltpu.make_async_copy(wout_hbm, wout_ref, sems.at[2]))
    for copy in copies:
        copy.start()
    copies[0].wait()
    text = text_ref[...].astype(F32)
    emb_ref[...] = (text * lax.rsqrt(jnp.sum(text * text, axis=-1, keepdims=True) + EPS)).astype(BF)
    copies[1].wait()
    for i, span in enumerate(spans):
        copies[2 + i].wait()
        pre = lax.dot_general(win_ref[span, :], feats_ref[...], NT, preferred_element_type=F32)
        hidden_ref[span, :] = gelu_val(pre, gelu_tanh(pre)).astype(BF)
        pre_ref[span, :] = pre.astype(BF)
    copies[-1].wait()
    partial_ref[...] = lax.dot_general(
        hidden_ref[...], wout_ref[...], (((0,), (0,)), ((), ())), preferred_element_type=F32
    ).astype(BF)


def feats_kernel(where_ref, feats_ref, own_ref, give_ref):
    x_index, c_index = where_ref[0], where_ref[1]
    rows, width = feats_ref.shape
    z_count = own_ref.shape[1] // LANES
    chunk = width // (4 * z_count)
    source = lax.broadcasted_iota(jnp.int32, (2 * LANES, LANES), 0)
    target = lax.broadcasted_iota(jnp.int32, (2 * LANES, LANES), 1)
    inside = (target >= OUT_COLS) & (target < OUT_COLS + chunk)
    for rx, rc in [(a, b) for a in range(2) for b in range(2)]:
        for z in range(z_count):
            target_z = lax.rem(where_ref[3] + z, z_count)
            begin = (((rx ^ x_index) * z_count + target_z) * 2 + (rc ^ c_index)) * chunk
            window = jnp.minimum(begin // LANES * LANES, width - 2 * LANES)
            shift = begin - window - OUT_COLS
            move = jnp.where(inside & (source == target + shift), 1.0, 0.0).astype(BF)
            piece = feats_ref[:, pl.ds(pl.multiple_of(window, LANES), 2 * LANES)]
            piece = jnp.dot(piece, move, preferred_element_type=F32).astype(BF)
            out_ref = (own_ref, give_ref)[rx]
            out_ref[rc * rows : (rc + 1) * rows, z * LANES : (z + 1) * LANES] = piece


def unit_kernel(got_ref, unit_ref, inv_ref, spread_ref):
    projected = jnp.sum(got_ref[...].astype(F32), axis=0)
    inv_norm = lax.rsqrt(jnp.sum(projected * projected, axis=-1, keepdims=True) + EPS)
    unit = projected * inv_norm
    unit_ref[...] = unit
    inv_ref[...] = jnp.broadcast_to(inv_norm, inv_ref.shape)
    spread_ref[...] = jnp.broadcast_to(unit.astype(BF)[None], spread_ref.shape)


def expo_block(scale_val, video_ref, text):
    count, own_rows, emb = video_ref.shape
    video = video_ref[...].reshape(count * own_rows, emb)
    return jnp.exp(scale_val * lax.dot_general(video, text, NT, preferred_element_type=F32))


def column_place(where_ref, block):
    return (((block // 2) ^ where_ref[0]) * 2 + ((block % 2) ^ where_ref[1])) * 2


def logits_kernel(where_ref, scale_ref, video_ref, *refs):
    text_refs, (spread_ref, col_ref) = refs[:4], refs[4:]
    for block in range(4):
        expo = expo_block(scale_ref[0], video_ref, text_refs[block][...])
        col_part = jnp.sum(expo, axis=0, keepdims=True)
        for half in range(2):
            col_ref[pl.ds(column_place(where_ref, block) + half, 1), :] = col_part[
                :, half * LANES : (half + 1) * LANES
            ]
    spread_ref[...] = jnp.broadcast_to(col_ref[...][None], spread_ref.shape)


def weights_kernel(where_ref, scale_ref, video_ref, *refs):
    text_refs, (got_ref, packed_ref, inv_ref) = refs[:4], refs[4:]
    count, own_rows, emb = video_ref.shape
    rows = count * own_rows
    col_sum = jnp.sum(got_ref[...], axis=0)
    logs = jnp.sum(jnp.sum(jnp.log(col_sum), axis=0, keepdims=True), axis=1, keepdims=True)
    logs = split3(logs)
    inv_ref[...] = 1.0 / col_sum
    first = jnp.zeros((rows, emb), F32)
    second = jnp.zeros((rows, emb), F32)
    row_part = jnp.zeros((rows, 1), F32)
    for block in range(4):
        text = text_refs[block][...]
        expo = expo_block(scale_ref[0], video_ref, text)
        row_part += jnp.sum(expo, axis=1, keepdims=True)
        place = column_place(where_ref, block)
        inv = jnp.concatenate([inv_ref[pl.ds(place + half, 1), :] for half in range(2)], axis=1)
        first += jnp.dot(expo.astype(BF), text, preferred_element_type=F32)
        second += jnp.dot((expo * inv).astype(BF), text, preferred_element_type=F32)
    tiles = emb // LANES
    for i, side in enumerate((first, second)):
        for tile in range(tiles):
            begin = (i * tiles + tile) * own_rows
            part = side[:, tile * LANES : (tile + 1) * LANES]
            packed_ref[:, begin : begin + own_rows, :] = part.astype(BF).reshape(count, own_rows, LANES)
    row_hi = row_part.astype(BF).astype(F32)
    row_lo = (row_part - row_hi).reshape(count, own_rows, 1)
    row_hi = row_hi.reshape(count, own_rows, 1)
    row = lax.broadcasted_iota(jnp.int32, (count, own_rows, LANES), 1)
    lane = lax.broadcasted_iota(jnp.int32, (count, own_rows, LANES), 2)
    turned = jnp.where(lane == row, row_hi, jnp.where(lane == row + own_rows, row_lo, 0.0))
    turned = jnp.sum(turned, axis=1, keepdims=True)
    row, lane = row[:, :EXTRA], lane[:, :EXTRA]
    extra = jnp.where(lane == 0, logs[0], jnp.where(lane == 1, logs[1], jnp.where(lane == 2, logs[2], 0.0)))
    extra = jnp.where(row == 0, turned, extra)
    packed_ref[:, 2 * tiles * own_rows :, :] = extra.astype(BF)


def proj_kernel(where_ref, scale_ref, back_ref, unit_ref, inv_ref, text_ref, out_ref, *, sharers):
    scale_val = scale_ref[0]
    own_rows, emb = unit_ref.shape
    back = jnp.sum(back_ref[...].astype(F32), axis=0)
    tiles = emb // LANES
    parts = [back[i * own_rows : (i + 1) * own_rows] for i in range(2 * tiles)]
    lane = lax.broadcasted_iota(jnp.int32, (own_rows, LANES), 1)
    row = lax.broadcasted_iota(jnp.int32, (own_rows, LANES), 0)
    sums = back[2 * tiles * own_rows : 2 * tiles * own_rows + 1]
    sums = jnp.where((lane == row) | (lane == row + own_rows), sums, 0.0)
    row_sum = jnp.sum(sums, axis=1, keepdims=True)
    weighted = jnp.concatenate(parts[:tiles], axis=1) / row_sum + jnp.concatenate(parts[tiles:], axis=1)
    text = text_ref[where_ref[2]].astype(F32)
    unit = unit_ref[...]
    positive = scale_val * jnp.sum(unit.astype(BF).astype(F32) * text, axis=-1, keepdims=True)
    rows_piece = jnp.sum(jnp.log(row_sum) - 2.0 * positive, axis=0, keepdims=True)
    logs = back[2 * tiles * own_rows + 1 : 2 * tiles * own_rows + 2]
    cols_piece = jnp.sum(logs, axis=1, keepdims=True)
    a, b, c = split3(rows_piece + cols_piece / sharers)
    grad_emb = 0.5 * scale_val * weighted - scale_val * text
    grad_proj = inv_ref[:, :1] * (
        grad_emb - unit * jnp.sum(unit * grad_emb, axis=-1, keepdims=True)
    )
    lane, row = lane[:EXTRA], row[:EXTRA]
    loss = jnp.where(lane == 0, a, jnp.where(lane == 1, b, jnp.where(lane == 2, c, 0.0)))
    loss = jnp.where(row == 0, loss, 0.0)
    sent = [grad_proj[:, i * LANES : (i + 1) * LANES] for i in range(tiles)]
    sent = jnp.concatenate(sent + [loss], axis=0).astype(BF)
    out_ref[...] = jnp.broadcast_to(sent[None], out_ref.shape)


def gelu_kernel(*refs):
    pre_refs, (hidden_ref, der_ref) = refs[:4], refs[4:]
    rows = pre_refs[0].shape[1]
    for block in range(4):
        pre = pre_refs[block][...].astype(F32)
        tanh_val = gelu_tanh(pre)
        span = slice(block * rows, (block + 1) * rows)
        hidden_ref[:, span] = gelu_val(pre, tanh_val).astype(BF)
        der_ref[:, span] = gelu_der(pre, tanh_val).astype(BF)


def grads_kernel(where_ref, own_hbm, other_hbm, wout_hbm, hidden_hbm, der_hbm, *refs):
    feats_hbm, out_refs, refs = refs[:4], refs[4:13], refs[13:]
    grads_ref, loss_ref, wout_ref, der_ref, hidden_ref, feats_ref, sems = refs
    x_index, c_index = where_ref[0], where_ref[1]
    _, mp_count, own_rows, _ = grads_ref.shape
    rows = mp_count * own_rows
    hid, emb = wout_ref.shape
    tiles = emb // LANES
    z_count = feats_ref.shape[1] // LANES
    spans = parts_of(hid, 2)
    copies = []
    for block in range(4):
        rx, rc = block // 2, block % 2
        source = other_hbm if rc else own_hbm
        source = source.at[rx ^ x_index]
        for tile in range(tiles):
            place = grads_ref.at[block, :, :, pl.ds(tile * LANES, LANES)]
            copies.append((source.at[:, pl.ds(tile * own_rows, own_rows), :], place))
        copies.append((source.at[:, pl.ds(tiles * own_rows, EXTRA), :], loss_ref.at[block]))
    ready = len(copies) + 1
    copies.append((wout_hbm, wout_ref))
    copies.append((der_hbm.at[spans[0]], der_ref.at[spans[0]]))
    for block in range(4):
        side = pl.ds(block % 2 * rows, rows)
        copies.append((feats_hbm[block].at[side], feats_ref.at[pl.ds(block * rows, rows)]))
    copies.append((hidden_hbm.at[spans[0]], hidden_ref.at[spans[0]]))
    copies.append((der_hbm.at[spans[1]], der_ref.at[spans[1]]))
    copies.append((hidden_hbm.at[spans[1]], hidden_ref.at[spans[1]]))
    copies = [pltpu.make_async_copy(a, b, sems.at[i]) for i, (a, b) in enumerate(copies)]
    for copy in copies:
        copy.start()
    source = lax.broadcasted_iota(jnp.int32, (emb, LANES), 0)
    target = lax.broadcasted_iota(jnp.int32, (emb, LANES), 1)
    column = lax.rem(where_ref[3] + target // OUT_COLS, z_count) * 2 + c_index
    column = x_index * (emb // 2) + column * OUT_COLS + target % OUT_COLS
    pick = jnp.where(source == column, 1.0, 0.0).astype(BF)
    for copy in copies[:ready]:
        copy.wait()
    grads = grads_ref[...].reshape(4 * rows, emb)
    picked = jnp.dot(grads, pick, preferred_element_type=F32).astype(BF)
    loss = jnp.zeros((1, LANES), F32)
    for block in range(4):
        part = loss_ref[block].reshape(mp_count * EXTRA, LANES).astype(F32)
        loss += jnp.sum(part, axis=0, keepdims=True)
    a, b, c = split3(jnp.sum(loss, axis=1, keepdims=True))
    for i, span in enumerate(spans):
        size = span.stop - span.start
        lane = lax.broadcasted_iota(jnp.int32, (size, LANES), 1)
        grad_hidden = lax.dot_general(wout_ref[span, :], grads, NT, preferred_element_type=F32)
        copies[ready + (0, 6)[i]].wait()
        grad_pre = (grad_hidden * der_ref[span, :].astype(F32)).astype(BF)
        if i == 0:
            for copy in copies[ready + 1 : ready + 5]:
                copy.wait()
        total = jnp.dot(grad_pre, feats_ref[...], preferred_element_type=F32)
        copies[ready + (5, 7)[i]].wait()
        outer = jnp.dot(hidden_ref[span, :], picked, preferred_element_type=F32)
        for z in range(z_count):
            moved = outer if z == 0 else pltpu.roll(outer, LANES - z * OUT_COLS, 1)
            value = jnp.where(lane < OUT_COLS, moved, total[:, z * LANES : (z + 1) * LANES])
            if i == 0:
                row = lax.broadcasted_iota(jnp.int32, (size, LANES), 0)
                extra = jnp.where(row == 0, a, jnp.where(row == 1, b, c))
                value = jnp.where((lane == LANES - 1) & (row < 3), extra, value)
            if z == FAR:
                out_refs[FAR + 4 * i][...] = value.astype(BF)
            else:
                out_refs[z][span, :] = value.astype(BF)


def near_kernel(up_ref, down_ref, up_far_ref, down_far_ref, up_out, down_out):
    first = up_far_ref.shape[0]
    up_out[:first] = (up_ref[:first].astype(F32) + up_far_ref[...].astype(F32)).astype(BF)
    up_out[first:] = up_ref[first:]
    down_out[:first] = down_ref[:first]
    down_out[first:] = (down_ref[first:].astype(F32) + down_far_ref[...].astype(F32)).astype(BF)


def final_kernel(*refs, batch_total):
    got, (in_ref, out_ref, loss_ref) = refs[:7], refs[7:]
    total = got[0][...].astype(F32)
    for ref in got[1:]:
        total += ref[...].astype(F32)
    turned = total.T
    in_rows = in_ref.shape[0]
    out_ref[...] = turned[:OUT_COLS]
    in_ref[...] = turned[OUT_COLS : OUT_COLS + in_rows]
    loss = jnp.sum(total[:3, LANES - 1 :], axis=0, keepdims=True) / (2.0 * batch_total)
    loss_ref[...] = loss


def ahead(value, step):
    return lax.ppermute(value, "z", [(i, (i + step) % 8) for i in range(8)])


def on_device(video_feats, text_feats, weight_in, weight_out, logit_scale):
    rows, d_in = video_feats.shape
    hid, emb = weight_out.shape
    mp_count = lax.axis_size(MP)
    own_rows = rows // mp_count
    packs = own_rows * (emb // LANES)
    batch_total = rows * lax.axis_size(DP)
    where = [lax.axis_index(name) for name in ("x_lo", "core", MP, "z")]
    where = jnp.stack(where).astype(jnp.int32)

    partial_value, pre_bf, text_emb = call(
        head_kernel, [((rows, emb), BF), ((hid, rows), BF), ((rows, emb), BF)], LIM[0],
        text_feats, video_feats, weight_in.T, weight_out, raw=True,
        scratch=[
            pltpu.VMEM((rows, emb), BF), pltpu.VMEM((rows, d_in), BF), pltpu.VMEM((hid, d_in), BF),
            pltpu.VMEM((hid, emb), BF), pltpu.VMEM((hid, rows), BF), pltpu.SemaphoreType.DMA((6,)),
        ],
    )
    got = exchange(partial_value.reshape(mp_count, own_rows, emb), MP)

    text_x = swap(text_emb, "x_lo")
    texts = [swap(text_emb, "core"), text_x, swap(text_x, "core")]
    z_count = lax.axis_size("z")
    feats, give_x = call(
        feats_kernel, [((2 * rows, z_count * LANES), BF)] * 2, LIM[1], where, video_feats, scalars=1
    )
    unit, inv_norm, video = call(
        unit_kernel,
        [((own_rows, emb), F32), ((own_rows, LANES), F32), ((8, own_rows, emb), BF)],
        LIM[2], got, after=(feats, text_x),
    )
    give_x, pre_own = gate(inv_norm, give_x, pre_bf)
    feats_x = swap(give_x, "x_lo")

    video_rows = exchange(video, "z")
    (cols,) = call(
        logits_kernel, [((4 * mp_count, 8, LANES), F32)], LIM[3],
        where, logit_scale, video_rows, text_emb, *texts, scalars=2, direct=True,
        scratch=[pltpu.VMEM((8, LANES), F32)],
    )
    cols = exchange(cols, PLANE)
    pre_x = swap(pre_own, "x_lo")
    pre = (pre_own, swap(pre_own, "core"), pre_x, swap(pre_x, "core"))
    (packed,) = call(
        weights_kernel, [((z_count, 2 * packs + EXTRA, LANES), BF)], LIM[4],
        where, logit_scale, video_rows, text_emb, *texts, cols, scalars=2, direct=True,
        scratch=[pltpu.VMEM((8, LANES), F32)],
    )
    feats_q = (feats, swap(feats, "core"), feats_x, swap(feats_x, "core"))
    back = exchange(packed, "z")
    (sent,) = call(
        functools.partial(proj_kernel, sharers=4 * mp_count * z_count),
        [((2 * mp_count, packs + EXTRA, LANES), BF)], LIM[5],
        where, logit_scale, back, unit, inv_norm, text_emb.reshape(mp_count, own_rows, emb),
        scalars=2, after=(feats_q[1], feats_q[3], pre[1], pre[3]),
    )
    gelus = call(gelu_kernel, [((hid, 4 * rows), BF)] * 2, LIM[6], *pre, after=(sent,))
    grads = exchange(sent, SPREAD).reshape(2, mp_count, packs + EXTRA, LANES)
    (grads,) = gate(gelus[0], grads, after=(gelus[1],))
    other = swap(grads, "core")
    first = parts_of(hid, 2)[0].stop
    sizes = [hid] * FAR + [first] + [hid] * (7 - FAR) + [hid - first]
    pieces = call(
        grads_kernel, [((size, LANES), BF) for size in sizes], LIM[7],
        where, grads, other, weight_out, *gelus, *feats_q, scalars=1, raw=True,
        scratch=[
            pltpu.VMEM((4, mp_count, own_rows, emb), BF), pltpu.VMEM((4, mp_count, EXTRA, LANES), BF),
            pltpu.VMEM((hid, emb), BF),
            pltpu.VMEM((hid, 4 * rows), BF), pltpu.VMEM((hid, 4 * rows), BF),
            pltpu.VMEM((4 * rows, z_count * LANES), BF), pltpu.SemaphoreType.DMA((29,)),
        ],
    )
    near = call(
        near_kernel, [((hid, LANES), BF)] * 2, LIM[9],
        pieces[3], pieces[5], ahead(pieces[FAR], 1), ahead(pieces[8], -1), direct=True,
    )
    final = [pieces[0], ahead(near[0], 3), ahead(near[1], -3)]
    final += [ahead(pieces[step], step) for step in (2, 6, 1, 7)]
    in_rows = d_in // lax.axis_size(DP)
    grad_in, grad_out, loss = call(
        functools.partial(final_kernel, batch_total=batch_total),
        [((in_rows, hid), F32), ((OUT_COLS, hid), F32), ((1, 1), F32)],
        LIM[8], *final, direct=True,
    )
    return (loss.reshape(1), grad_in, grad_out.T)


def solution(mesh):
    fine = Mesh(mesh.devices.reshape(2, -1, 2, mesh.devices.shape[1] // 2, 2), DP + MP)
    in_specs = (P(DP, None), P(DP, None), P(None, MP), P(MP, None), P())
    out_specs = (P(), P(DP, MP), P(MP, DP))
    return jax.shard_map(
        on_device, mesh=fine, in_specs=in_specs, out_specs=out_specs, check_vma=False
    )
```
